32 devices in a mesh: row: 4 (over y, core), col: 8 (over z, x).
Axes of the slice: x: 2, y: 2, z: 4, core: 2. Of those that a mesh axis runs over, the one named last changes fastest.
Arguments:
- inverse_block: bfloat16 [4096, 4096], P('row', 'col'), may hold values from -0.75 to 0.75
- tile_mask: int32 [32, 32], P('row', 'col'), may hold values 0 or 1
- factor: bfloat16 [2, 4096, 256], P(None, 'row'), may hold values from -0.29882812 to 0.29882812
- panel_mask: int32 [2, 32], P(None, 'row'), may hold values 0 or 1
- child_top: bfloat16 [256, 256], replicated, may hold values from -0.375 to 0.375
- pivots: float32 [2, 256, 256], replicated, may hold values from -6 to 6
Outputs:
- parent_column: float32 [4096, 256], P(('row', 'col'))
- parent_diag: float32 [256, 256], replicated
- child_upper: float32 [256, 256], replicated
- child_column: float32 [4096, 256], P(('row', 'col'))
- child_diag: float32 [256, 256], replicated
The draws below stay inside these ranges and needn't reach their ends.
All inputs are finite; a program needn't handle non-finite values. No bound on the sum of `tile_mask` or of `panel_mask` on one device may be relied on, other than what follows from the above.
Results may differ from the reference program's by a relative error of at most 0.0003.
Values may be sent and summed in bfloat16 or wider, within the bound.
A program may use at most 64 MiB of HBM per device.

```python
import jax
import jax.numpy as jnp
from jax import lax

W = 256
BLOCK = 128
R = 4096


def set_ends(array, stream_key, smallest, largest):
    extent = array.shape
    place = [jax.random.randint(jax.random.fold_in(stream_key, axis), (), 0, extent[axis]) for axis in range(len(extent))]
    array = array.at[tuple(place)].set(smallest)
    longest = extent.index(max(extent))
    place[longest] = (place[longest] + 1) % extent[longest]
    return array.at[tuple(place)].set(largest)


def block_scale(stream_key, shape, split, smallest, largest):
    def one(position, parts):
        draws = jax.random.uniform(jax.random.fold_in(jax.random.fold_in(stream_key, 6), position), (parts,), jnp.float32, smallest / len(split), largest / len(split))
        return jnp.repeat(jnp.exp(draws), shape[position] // parts).reshape((-1,) + (1,) * (len(shape) - position - 1))

    factor_of = one(*split[0])
    for cut in split[1:]:
        factor_of = factor_of * one(*cut)
    return factor_of


def centred(own_key, extent, scale, reach, shards=(), held_as=jnp.bfloat16):
    loudness = block_scale(own_key, extent, shards, -0.22, 0.18) if shards else 1.0
    result = jax.random.normal(own_key, extent, jnp.float32) * scale * loudness
    return jnp.minimum(jnp.maximum(result, -reach), reach).astype(held_as)


def setup_inputs(seed: int = 0) -> dict:
    key_list = jax.random.split(jax.random.key(seed), 7)
    return {
        "inverse_block": centred(key_list[0], (R, R), (R // 64) ** -0.5, 0.75, ((0, 4), (1, 8))),
        "tile_mask": set_ends((jax.random.randint(key_list[1], (R // BLOCK, R // BLOCK), 0, 5) < 3).astype(jnp.int32), jax.random.fold_in(key_list[1], 1), 0, 1),
        "factor": centred(key_list[2], (2, R, W), 0.05, 0.29882812, ((1, 4),)),
        "panel_mask": set_ends((jax.random.randint(key_list[3], (2, R // BLOCK), 0, 5) < 3).astype(jnp.int32), jax.random.fold_in(key_list[3], 1), 0, 1),
        "child_top": centred(key_list[4], (W, W), W ** -0.5, 0.375),
        "pivots": centred(key_list[5], (2, W, W), 1.0, 6.0, (), jnp.float32),
    }


def reference(inverse_block, tile_mask, factor, panel_mask, child_top, pivots):
    total_rows = inverse_block.shape[0]
    panel_width = factor.shape[2]
    nblocks = total_rows // 128
    keep_panel = panel_mask.astype(jnp.bfloat16)
    panels = (factor.reshape(2, nblocks, 128, panel_width) * keep_panel[:, :, None, None]).reshape(2, total_rows, panel_width)
    joined_panels = jnp.concatenate([panels[0], panels[1]], axis=1)
    slab_rows = 1024
    slab_count = total_rows // slab_rows

    def one_slab(slab_index):
        slab = lax.dynamic_slice_in_dim(inverse_block, slab_index * slab_rows, slab_rows, 0)
        slab_mask = lax.dynamic_slice_in_dim(tile_mask, slab_index * (slab_rows // 128), slab_rows // 128, 0)
        masked = (slab.reshape(slab_rows // 128, 128, nblocks, 128) * slab_mask.astype(jnp.bfloat16)[:, None, :, None]).reshape(slab_rows, total_rows)
        return jnp.dot(masked, joined_panels, preferred_element_type=jnp.float32)

    products = lax.map(one_slab, jnp.arange(slab_count, dtype=jnp.int32)).reshape(total_rows, 2 * panel_width)
    highest = lax.Precision.HIGHEST
    panel_zero = panels[0].astype(jnp.float32)
    panel_one = panels[1].astype(jnp.float32)
    top_float = child_top.astype(jnp.float32)
    parent_column = -products[:, :panel_width]
    parent_diag = pivots[0] - jnp.dot(panel_zero.T, parent_column, precision=highest)
    child_upper = -(jnp.dot(parent_diag, top_float, precision=highest) + jnp.dot(parent_column.T, panel_one, precision=highest))
    child_column = -(jnp.dot(parent_column, top_float, precision=highest) + products[:, panel_width:])
    child_diag = pivots[1] - jnp.dot(top_float.T, child_upper, precision=highest) - jnp.dot(panel_one.T, child_column, precision=highest)
    return parent_column, parent_diag, child_upper, child_column, child_diag
```

```python
import functools

import jax
import jax.numpy as jnp
from jax import lax
from jax.experimental import pallas as pl
from jax.experimental.pallas import tpu as pltpu
from jax.sharding import PartitionSpec as P

BLOCK = 128
MESH = pl.DeviceIdType.MESH
F32 = jnp.float32
BF16 = jnp.bfloat16


def split(a):
    high = a.astype(BF16)
    return high, (a - high.astype(F32)).astype(BF16)


def dot(a, b):
    return jnp.dot(a, b, preferred_element_type=F32)


def dot_t(a, b):
    return lax.dot_general(a, b, (((0,), (0,)), ((), ())), preferred_element_type=F32)


def kernel(
    nr, nc, m_ref, tm_ref, f_ref, pm_ref, top_ref, piv_ref,
    pc_ref, pd_ref, cu_ref, cc_ref, cd_ref,
    mk, jown, jz, mx, q, zs, zr, gp, gr, gc, gown, gfull,
    ps_sem, pr_sem, fs_sem, ms_sem, mr_sem, zs_sem, zr_sem,
    as_sem, ar_sem, bs_sem, br_sem, cs_sem, cr_sem, ds_sem, dr_sem,
):
    r, c = lax.axis_index("row"), lax.axis_index("col")
    ratio = nc // nr
    rows, cols = m_ref.shape
    width = f_ref.shape[2]
    kr = rows // nc
    qr = cols // 2
    grows = gp.shape[0] // nr
    gcols = gown.shape[0]
    shared = gc.shape[0] == nc
    x, z = lax.rem(c, ratio), lax.div(c, ratio)
    chip, core = lax.div(r, 2), lax.rem(r, 2)
    chips = nr // 2
    mate = chip * 2 + 1 - core
    is_source = r == z
    same_chip = chip == lax.div(z, 2)
    sent = []

    def copy(src, dst, send, recv, row, col):
        return pltpu.make_async_remote_copy(
            src_ref=src, dst_ref=dst, send_sem=send, recv_sem=recv,
            device_id=(row, col), device_id_type=MESH,
        )

    def start(src, dst, send, recv, row, col):
        made = copy(src, dst, send, recv, row, col)
        made.start()
        sent.append(made)

    def arrived(dst, send, recv):
        copy(dst, dst, send, recv, r, c).wait_recv()

    def at(ref, first, count):
        return ref.at[pl.ds(pl.multiple_of(first, 16), count)]

    barrier = pltpu.get_barrier_semaphore()
    for d in range(1, nr):
        pl.semaphore_signal(
            barrier, inc=1, device_id=(lax.rem(r + d, nr), c), device_id_type=MESH
        )
    for d in range(1, nc):
        pl.semaphore_signal(
            barrier, inc=1, device_id=(r, lax.rem(c + d, nc)), device_id_type=MESH
        )
    for b in range(rows // BLOCK):
        part = slice(b * BLOCK, (b + 1) * BLOCK)
        for s in range(2):
            keep = pm_ref[s, b].astype(F32)
            jown[part, s * width : (s + 1) * width] = (f_ref[s, part, :].astype(F32) * keep).astype(BF16)
    pl.semaphore_wait(barrier, nr + nc - 2)

    def piece(ref, e, h):
        half = lax.rem(x + e, ratio)
        return at(ref, (half * 2 + h) * qr, qr)

    def panel_copies(e):
        made = []
        for h in range(2):
            i = 2 * e + h
            made.append(
                copy(piece(jown, e, h), piece(jz, e, h), ps_sem.at[i, 0], pr_sem.at[i], mate, c)
            )
            for d in range(1, chips):
                to = lax.rem(chip + d, chips) * 2 + h
                made.append(
                    copy(piece(jown, e, h), piece(jz, e, h), ps_sem.at[i, d], pr_sem.at[i], to, c)
                )
        return made

    def forward_copy(e):
        half = lax.rem(x + e, ratio)
        part = at(jz, (half * 2 + core) * qr, qr)
        i = 2 * e + core
        return part, copy(part, part, fs_sem.at[e], pr_sem.at[i], mate, c)

    def panels_arrive(e):
        @pl.when(jnp.logical_and(jnp.logical_not(is_source), same_chip))
        def _():
            for h in range(2):
                arrived(piece(jz, e, h), ps_sem.at[2 * e + h, 0], pr_sem.at[2 * e + h])

        @pl.when(jnp.logical_not(same_chip))
        def _():
            part, made = forward_copy(e)
            arrived(part, fs_sem.at[e], pr_sem.at[2 * e + core])
            made.start()
            half = lax.rem(x + e, ratio)
            other = at(jz, (half * 2 + 1 - core) * qr, qr)
            arrived(other, fs_sem.at[e], pr_sem.at[2 * e + 1 - core])

    @pl.when(is_source)
    def _():
        for made in panel_copies(0):
            made.start()
        jz[...] = jown[...]

    for b in range(rows // BLOCK):
        for j in range(cols // BLOCK):
            tile = (slice(b * BLOCK, (b + 1) * BLOCK), slice(j * BLOCK, (j + 1) * BLOCK))
            mk[tile] = (m_ref[tile].astype(F32) * tm_ref[b, j].astype(F32)).astype(BF16)
    for e in range(nr):
        g = lax.rem(z + 1 + e, nr)
        for d in range(1, ratio):
            xx = lax.rem(x + d, ratio)
            start(
                at(mk, (g * ratio + xx) * kr, kr), mx.at[d - 1, e],
                ms_sem.at[d - 1, e], mr_sem.at[d - 1, e], r, z * ratio + xx,
            )

    panels_arrive(0)
    near = jz[pl.ds(pl.multiple_of(x * cols, cols), cols), :]
    step = min(rows, 256)
    for b in range(rows // step):
        part = slice(b * step, (b + 1) * step)
        q[part, :] = dot(mk[part, :], near)

    @pl.when(is_source)
    def _():
        for e in range(1, ratio):
            for made in panel_copies(e):
                made.start()

    for j in range(2 * width // BLOCK):
        left = 0 if j * BLOCK < width else width
        high, low = split(q[:, j * BLOCK : (j + 1) * BLOCK])
        own = jown[:, left:]
        value = dot_t(own, high) + dot_t(own, low)
        slots = width // BLOCK
        if left == 0:
            gp[j * width : (j + 1) * width, :] = value[:width]
            gp[(slots + j) * width : (slots + j + 1) * width, :] = value[width:]
        else:
            gp[(slots + j) * width : (slots + j + 1) * width, :] = value
    for d in range(1, nr):
        to = lax.rem(r + d, nr)
        start(at(gp, to * grows, grows), gr.at[d - 1], as_sem.at[d - 1], ar_sem.at[d - 1], to, c)
    total = gp[pl.ds(pl.multiple_of(r * grows, 16), grows), :]
    for d in range(1, nr):
        arrived(gr.at[d - 1], as_sem.at[d - 1], ar_sem.at[d - 1])
        total = total + gr[d - 1]
    if shared:
        gc[pl.ds(c, 1)] = total[None]
        for d in range(1, nc):
            to = lax.rem(c + d, nc)
            start(gc.at[c], gc.at[c], bs_sem.at[d - 1], br_sem.at[d - 1], r, to)
    else:
        gr[nr - 1] = total
        for d in range(1, nc):
            to = lax.rem(c + d, nc)
            start(
                gr.at[nr - 1, pl.ds(pl.multiple_of(to * gcols, 16), gcols)], gc.at[d - 1],
                bs_sem.at[d - 1], br_sem.at[d - 1], r, to,
            )

    for e in range(1, ratio):
        panels_arrive(e)
    for e in range(nr):
        g = lax.rem(z + 1 + e, nr)
        value = q[pl.ds(pl.multiple_of((g * ratio + x) * kr, 16), kr), :]
        for d in range(1, ratio):
            arrived(mx.at[d - 1, e], ms_sem.at[d - 1, e], mr_sem.at[d - 1, e])
            half = lax.rem(x - d + ratio, ratio)
            value = value + dot(mx[d - 1, e], jz[pl.ds(pl.multiple_of(half * cols, cols), cols), :])
        zs[e] = value
        if e < nr - 1:
            start(zs.at[e], zr.at[e], zs_sem.at[e], zr_sem.at[e], r, g * ratio + x)

    if shared:
        for d in range(1, nc):
            come = lax.rem(c - d + nc, nc)
            arrived(gc.at[come], bs_sem.at[d - 1], br_sem.at[d - 1])
        total = gc[0]
        for i in range(1, nc):
            total = total + gc[i]
        gfull[pl.ds(pl.multiple_of(r * grows, 16), grows), :] = total
    else:
        total = gr[nr - 1, pl.ds(pl.multiple_of(c * gcols, 16), gcols), :]
        for d in range(1, nc):
            arrived(gc.at[d - 1], bs_sem.at[d - 1], br_sem.at[d - 1])
            total = total + gc[d - 1]
        mine = r * grows + c * gcols
        gfull[pl.ds(pl.multiple_of(mine, 16), gcols), :] = total
        for d in range(1, nc):
            to = lax.rem(c + d, nc)
            start(
                at(gfull, mine, gcols), at(gfull, mine, gcols),
                cs_sem.at[d - 1], cr_sem.at[d - 1], r, to,
            )
        for d in range(1, nc):
            come = lax.rem(c - d + nc, nc)
            arrived(at(gfull, r * grows + come * gcols, gcols), cs_sem.at[d - 1], cr_sem.at[d - 1])
    for d in range(1, nr):
        to = lax.rem(r + d, nr)
        block = at(gfull, r * grows, grows)
        start(block, block, ds_sem.at[d - 1], dr_sem.at[d - 1], to, c)

    top = top_ref[...]
    value = zs[nr - 1]
    for e in range(nr - 1):
        arrived(zr.at[e], zs_sem.at[e], zr_sem.at[e])
        value = value + zr[e]
    parent = value[:, :width]
    high, low = split(parent)
    pc_ref[...] = -parent
    cc_ref[...] = dot(high, top) + dot(low, top) - value[:, width:]

    for d in range(1, nr):
        come = lax.rem(r - d + nr, nr)
        arrived(at(gfull, come * grows, grows), ds_sem.at[d - 1], dr_sem.at[d - 1])
    slots = width // BLOCK

    def square(i):
        return jnp.concatenate(
            [gfull[(i * slots + j) * width : (i * slots + j + 1) * width, :] for j in range(slots)], axis=1
        )

    diag = piv_ref[0] + square(0)
    pd_ref[...] = diag
    cross = square(1)
    high, low = split(diag)
    upper = cross.T - (dot(high, top) + dot(low, top))
    cu_ref[...] = upper
    high, low = split(upper)
    cross_high, cross_low = split(cross)
    cd_ref[...] = (
        piv_ref[1] - (dot_t(top, high) + dot_t(top, low))
        - (dot(cross_high, top) + dot(cross_low, top)) + square(2)
    )

    for made in sent:
        made.wait_send()

    @pl.when(is_source)
    def _():
        for e in range(ratio):
            for made in panel_copies(e):
                made.wait_send()

    @pl.when(jnp.logical_not(same_chip))
    def _():
        for e in range(ratio):
            forward_copy(e)[1].wait_send()


def shards(nr, nc, inverse_block, tile_mask, factor, panel_mask, child_top, pivots):
    rows, cols = inverse_block.shape
    width = factor.shape[2]
    ratio = nc // nr
    kr = rows // nc
    small = 3 * width * width // BLOCK
    grows = small // nr
    shared = grows % (16 * nc) != 0
    gcols = 16 if shared else grows // nc
    dma = pltpu.SemaphoreType.DMA
    vmem, smem = pl.BlockSpec(memory_space=pltpu.VMEM), pl.BlockSpec(memory_space=pltpu.SMEM)
    square = jax.ShapeDtypeStruct((width, width), F32)
    column = jax.ShapeDtypeStruct((kr, width), F32)
    return pl.pallas_call(
        functools.partial(kernel, nr, nc),
        out_shape=(column, square, square, column, square),
        in_specs=[vmem, smem, vmem, smem, vmem, vmem],
        out_specs=(vmem,) * 5,
        scratch_shapes=[
            pltpu.VMEM((rows, cols), BF16),
            pltpu.VMEM((rows, 2 * width), BF16),
            pltpu.VMEM((rows, 2 * width), BF16),
            pltpu.VMEM((max(ratio - 1, 1), nr, kr, cols), BF16),
            pltpu.VMEM((rows, 2 * width), F32),
            pltpu.VMEM((nr, kr, 2 * width), F32),
            pltpu.VMEM((nr - 1, kr, 2 * width), F32),
            pltpu.VMEM((small, BLOCK), F32),
            pltpu.VMEM((nr, grows, BLOCK), F32),
            pltpu.VMEM((nc, grows, BLOCK) if shared else (nc - 1, gcols, BLOCK), F32),
            pltpu.VMEM((gcols, BLOCK), F32),
            pltpu.VMEM((small, BLOCK), F32),
            dma((2 * ratio, max(nr // 2, 1))), dma((2 * ratio,)), dma((ratio,)),
            dma((max(ratio - 1, 1), nr)), dma((max(ratio - 1, 1), nr)),
            dma((nr - 1,)), dma((nr - 1,)),
            dma((nr - 1,)), dma((nr - 1,)),
            dma((nc - 1,)), dma((nc - 1,)),
            dma((nc - 1,)), dma((nc - 1,)),
            dma((nr - 1,)), dma((nr - 1,)),
        ],
        compiler_params=pltpu.CompilerParams(
            collective_id=0, has_side_effects=True, vmem_limit_bytes=40 * 1024 * 1024
        ),
    )(inverse_block, tile_mask, factor, panel_mask, child_top, pivots)


def solution(mesh):
    in_specs = (P("row", "col"), P("row", "col"), P(None, "row", None), P(None, "row"), P(), P())
    out_specs = (P(("row", "col"), None), P(), P(), P(("row", "col"), None), P())
    body = functools.partial(shards, mesh.shape["row"], mesh.shape["col"])
    return jax.shard_map(body, mesh=mesh, in_specs=in_specs, out_specs=out_specs, check_vma=False)
```

```python
import functools

import jax
import jax.numpy as jnp
from jax import lax
from jax.experimental import pallas as pl
from jax.experimental.pallas import tpu as pltpu
from jax.sharding import PartitionSpec as P

BLOCK = 128
GROUP = 16
MESH = pl.DeviceIdType.MESH
F32 = jnp.float32
BF16 = jnp.bfloat16


def split(a):
    high = a.astype(BF16)
    return high, (a - high.astype(F32)).astype(BF16)


def dot(a, b):
    return jnp.dot(a, b, preferred_element_type=F32)


def dot_t(a, b):
    return lax.dot_general(a, b, (((0,), (0,)), ((), ())), preferred_element_type=F32)


def quantize(a):
    groups = a.shape[0] // GROUP
    parts = a.reshape(groups, GROUP, a.shape[1])
    largest = jnp.maximum(jnp.max(jnp.abs(parts), axis=1), 1e-30)
    whole = jnp.round(parts * (32767.0 / largest)[:, None, :]).astype(jnp.int32)
    return whole.reshape(a.shape).astype(jnp.int16), largest * (1.0 / 32767.0)


def restore(whole, scale):
    groups = whole.shape[0] // GROUP
    parts = whole.astype(jnp.int32).astype(F32).reshape(groups, GROUP, whole.shape[1])
    return (parts * scale[:groups][:, None, :]).reshape(whole.shape)


def kernel(
    nr, nc, m_any, tm_any, f_any, pm_any, sum_ref, g_ref,
    m_ref, tm_ref, f_ref, pm_ref, mk, jown, jt, jz, mx, q, own, zq, zx, zrq, zrx, gp,
    gpq, gps, grq, grs, gtq, gts, gcq, gcs, gfq, gfs, in_sem,
    ps_sem, pr_sem, fs_sem, ms_sem, mr_sem, zs_sem, zr_sem,
    as_sem, ar_sem, bs_sem, br_sem, cs_sem, cr_sem, ds_sem, dr_sem,
):
    r, c = lax.axis_index("row"), lax.axis_index("col")
    ratio = nc // nr
    rows, cols = m_ref.shape
    width = f_ref.shape[2]
    kr = rows // nc
    qr = cols // 2
    grows = gp.shape[0] // nr
    lots = gfs.shape[1]
    shared = lots == 1
    gcols = grows // lots
    x, z = lax.rem(c, ratio), lax.div(c, ratio)
    chip, core = lax.div(r, 2), lax.rem(r, 2)
    chips = nr // 2
    mate = chip * 2 + 1 - core
    is_source = r == z
    same_chip = chip == lax.div(z, 2)
    sent = []

    loads = [
        pltpu.make_async_copy(there, here, in_sem.at[i])
        for i, (there, here) in enumerate(
            ((pm_any, pm_ref), (f_any, f_ref), (tm_any, tm_ref), (m_any, m_ref))
        )
    ]
    for load in loads:
        load.start()

    def copy(src, dst, send, recv, row, col):
        return pltpu.make_async_remote_copy(
            src_ref=src, dst_ref=dst, send_sem=send, recv_sem=recv,
            device_id=(row, col), device_id_type=MESH,
        )

    def start(src, dst, send, recv, row, col):
        made = copy(src, dst, send, recv, row, col)
        made.start()
        sent.append(made)

    def arrived(dst, send, recv):
        copy(dst, dst, send, recv, r, c).wait_recv()

    def at(ref, first, count):
        return ref.at[pl.ds(pl.multiple_of(first, 16), count)]

    barrier = pltpu.get_barrier_semaphore()
    for d in range(1, nr):
        pl.semaphore_signal(
            barrier, inc=1, device_id=(lax.rem(r + d, nr), c), device_id_type=MESH
        )
    for d in range(1, nc):
        pl.semaphore_signal(
            barrier, inc=1, device_id=(r, lax.rem(c + d, nc)), device_id_type=MESH
        )
    loads[0].wait()
    loads[1].wait()
    for b in range(rows // BLOCK):
        part = slice(b * BLOCK, (b + 1) * BLOCK)
        for s in range(2):
            keep = pm_ref[s : s + 1, b : b + 1].astype(F32)
            jown[part, s * width : (s + 1) * width] = (f_ref[s, part, :].astype(F32) * keep).astype(BF16)
    pl.semaphore_wait(barrier, nr + nc - 2)

    def piece(ref, e, h):
        half = lax.rem(x + e, ratio)
        return at(ref, (half * 2 + h) * qr, qr)

    def panel_copies(e):
        made = []
        for h in range(2):
            i = 2 * e + h
            for d in range(1, chips):
                to = lax.rem(chip + d, chips) * 2 + h
                made.append(
                    copy(piece(jown, e, h), piece(jz, e, h), ps_sem.at[i, d], pr_sem.at[i], to, c)
                )
            made.append(
                copy(piece(jown, e, h), piece(jz, e, h), ps_sem.at[i, 0], pr_sem.at[i], mate, c)
            )
        return made

    def forward_copy(e):
        half = lax.rem(x + e, ratio)
        part = at(jz, (half * 2 + core) * qr, qr)
        i = 2 * e + core
        return part, copy(part, part, fs_sem.at[e], pr_sem.at[i], mate, c)

    def panels_arrive(e):
        @pl.when(jnp.logical_and(jnp.logical_not(is_source), same_chip))
        def _():
            for h in range(2):
                arrived(piece(jz, e, h), ps_sem.at[2 * e + h, 0], pr_sem.at[2 * e + h])

        @pl.when(jnp.logical_not(same_chip))
        def _():
            part, made = forward_copy(e)
            arrived(part, fs_sem.at[e], pr_sem.at[2 * e + core])
            made.start()
            half = lax.rem(x + e, ratio)
            other = at(jz, (half * 2 + 1 - core) * qr, qr)
            arrived(other, fs_sem.at[e], pr_sem.at[2 * e + 1 - core])

    @pl.when(is_source)
    def _():
        for made in panel_copies(0):
            made.start()

    loads[2].wait()
    loads[3].wait()
    for b in range(rows // BLOCK):
        for j in range(cols // BLOCK):
            tile = (slice(b * BLOCK, (b + 1) * BLOCK), slice(j * BLOCK, (j + 1) * BLOCK))
            keep = tm_ref[b : b + 1, j : j + 1].astype(F32)
            mk[tile] = (m_ref[tile].astype(F32) * keep).astype(BF16)
    for e in range(nr):
        g = lax.rem(z + 1 + e, nr)
        for d in range(1, ratio):
            xx = lax.rem(x + d, ratio)
            start(
                at(mk, (g * ratio + xx) * kr, kr), mx.at[d - 1, e],
                ms_sem.at[d - 1, e], mr_sem.at[d - 1, e], r, z * ratio + xx,
            )

    jt[...] = jown[...].T

    @pl.when(is_source)
    def _():
        jz[...] = jown[...]
        for made in panel_copies(0):
            made.wait_send()
        for e in range(1, ratio):
            for made in panel_copies(e):
                made.start()

    panels_arrive(0)
    near = jz[pl.ds(pl.multiple_of(x * cols, cols), cols), :]
    step = min(rows, 256)
    for b in range(rows // step):
        part = slice(b * step, (b + 1) * step)
        q[part, :] = dot(mk[part, :], near)

    slots = width // BLOCK
    for s in range(2):
        high, low = split(q[:, s * width : (s + 1) * width])
        turned = jt[s * width :, :]
        value = dot(turned, high) + dot(turned, low)
        for i in range(2 - s):
            for j in range(slots):
                first = ((i + 2 * s) * slots + j) * width
                gp[first : first + width, :] = value[
                    i * width : (i + 1) * width, j * BLOCK : (j + 1) * BLOCK
                ]
    glines = grows // GROUP
    for i in range(nr):
        part = slice(i * grows, (i + 1) * grows)
        gpq[part, :], gps[i, :glines, :] = quantize(gp[part, :])
    for d in range(1, nr):
        to = lax.rem(r + d, nr)
        start(gps.at[to], grs.at[d - 1], as_sem.at[1, d - 1], ar_sem.at[1, d - 1], to, c)
        start(at(gpq, to * grows, grows), grq.at[d - 1], as_sem.at[0, d - 1], ar_sem.at[0, d - 1], to, c)
    total = gp[pl.ds(pl.multiple_of(r * grows, 16), grows), :]
    for d in range(1, nr):
        arrived(grs.at[d - 1], as_sem.at[1, d - 1], ar_sem.at[1, d - 1])
        arrived(grq.at[d - 1], as_sem.at[0, d - 1], ar_sem.at[0, d - 1])
        total = total + restore(grq[d - 1], grs[d - 1])
    gp[pl.ds(pl.multiple_of(r * grows, 16), grows), :] = total
    lines = gcols // GROUP
    for i in range(lots):
        part = slice(i * gcols, (i + 1) * gcols)
        gtq[part, :], gts[i, :lines, :] = quantize(total[part, :])
    for d in range(1, nc):
        to = lax.rem(c + d, nc)
        place = 0 if shared else to
        start(gts.at[place], gcs.at[c], bs_sem.at[1, d - 1], br_sem.at[1, d - 1], r, to)
        start(at(gtq, place * gcols, gcols), gcq.at[c], bs_sem.at[0, d - 1], br_sem.at[0, d - 1], r, to)
    place = 0 if shared else c
    gcs[pl.ds(c, 1)] = gts[pl.ds(place, 1)]
    gcq[pl.ds(c, 1)] = gtq[pl.ds(pl.multiple_of(place * gcols, 16), gcols), :][None]

    for e in range(1, ratio):
        panels_arrive(e)
    zlines = kr // GROUP
    for e in range(nr):
        g = lax.rem(z + 1 + e, nr)
        value = q[pl.ds(pl.multiple_of((g * ratio + x) * kr, 16), kr), :]
        for d in range(1, ratio):
            arrived(mx.at[d - 1, e], ms_sem.at[d - 1, e], mr_sem.at[d - 1, e])
            half = lax.rem(x - d + ratio, ratio)
            value = value + dot(mx[d - 1, e], jz[pl.ds(pl.multiple_of(half * cols, cols), cols), :])
        if e < nr - 1:
            zq[e], zx[e, :zlines, :] = quantize(value)
            to = g * ratio + x
            start(zx.at[e], zrx.at[e], zs_sem.at[1, e], zr_sem.at[1, e], r, to)
            start(zq.at[e], zrq.at[e], zs_sem.at[0, e], zr_sem.at[0, e], r, to)
        else:
            own[...] = value

    total = None
    for d in range(1, nc):
        come = lax.rem(c + nc - d, nc)
        arrived(gcs.at[come], bs_sem.at[1, d - 1], br_sem.at[1, d - 1])
        arrived(gcq.at[come], bs_sem.at[0, d - 1], br_sem.at[0, d - 1])
    for i in range(nc):
        value = restore(gcq[i], gcs[i])
        total = value if total is None else total + value
    mine = r * grows + place * gcols
    whole, scale = quantize(total)
    gfq[pl.ds(pl.multiple_of(mine, 16), gcols), :] = whole
    padding = gfs.shape[2] - lines
    if padding:
        scale = jnp.concatenate([scale, jnp.zeros((padding, BLOCK), F32)], axis=0)
    gfs[r, place] = scale
    if not shared:
        for d in range(1, nc):
            to = lax.rem(c + d, nc)
            start(gfs.at[r, c], gfs.at[r, c], cs_sem.at[1, d - 1], cr_sem.at[1, d - 1], r, to)
            block = at(gfq, mine, gcols)
            start(block, block, cs_sem.at[0, d - 1], cr_sem.at[0, d - 1], r, to)
        for d in range(1, nc):
            come = lax.rem(c + nc - d, nc)
            arrived(gfs.at[r, come], cs_sem.at[1, d - 1], cr_sem.at[1, d - 1])
            arrived(at(gfq, r * grows + come * gcols, gcols), cs_sem.at[0, d - 1], cr_sem.at[0, d - 1])
    for d in range(1, nr):
        to = lax.rem(r + d, nr)
        start(gfs.at[r], gfs.at[r], ds_sem.at[1, d - 1], dr_sem.at[1, d - 1], to, c)
        block = at(gfq, r * grows, grows)
        start(block, block, ds_sem.at[0, d - 1], dr_sem.at[0, d - 1], to, c)

    value = own[...]
    for e in range(nr - 1):
        arrived(zrx.at[e], zs_sem.at[1, e], zr_sem.at[1, e])
        arrived(zrq.at[e], zs_sem.at[0, e], zr_sem.at[0, e])
        value = value + restore(zrq[e], zrx[e])
    sum_ref[...] = value

    for d in range(1, nr):
        come = lax.rem(r + nr - d, nr)
        arrived(gfs.at[come], ds_sem.at[1, d - 1], dr_sem.at[1, d - 1])
        arrived(at(gfq, come * grows, grows), ds_sem.at[0, d - 1], dr_sem.at[0, d - 1])
    for i in range(nr):
        for j in range(lots):
            part = slice(i * grows + j * gcols, i * grows + (j + 1) * gcols)
            g_ref[part, :] = restore(gfq[part, :], gfs[i, j])

    for made in sent:
        made.wait_send()

    @pl.when(is_source)
    def _():
        for e in range(1, ratio):
            for made in panel_copies(e):
                made.wait_send()

    @pl.when(jnp.logical_not(same_chip))
    def _():
        for e in range(ratio):
            forward_copy(e)[1].wait_send()


def finish(sum_ref, g_ref, top_ref, piv_ref, pc_ref, pd_ref, cu_ref, cc_ref, cd_ref):
    width = top_ref.shape[0]
    slots = width // BLOCK
    top = top_ref[...]
    value = sum_ref[...]
    parent = value[:, :width]
    high, low = split(parent)
    pc_ref[...] = -parent
    cc_ref[...] = dot(high, top) + dot(low, top) - value[:, width:]

    def square(i):
        return jnp.concatenate(
            [g_ref[(i * slots + j) * width : (i * slots + j + 1) * width, :] for j in range(slots)], axis=1
        )

    diag = piv_ref[0] + square(0)
    pd_ref[...] = diag
    cross = square(1)
    high, low = split(diag)
    upper = cross.T - (dot(high, top) + dot(low, top))
    cu_ref[...] = upper
    high, low = split(upper)
    cross_high, cross_low = split(cross)
    cd_ref[...] = (
        piv_ref[1] - (dot_t(top, high) + dot_t(top, low))
        - (dot(cross_high, top) + dot(cross_low, top)) + square(2)
    )


def eights(count):
    return -(-count // 8) * 8


def shards(nr, nc, inverse_block, tile_mask, factor, panel_mask, child_top, pivots):
    rows, cols = inverse_block.shape
    width = factor.shape[2]
    ratio = nc // nr
    kr = rows // nc
    small = 3 * width * width // BLOCK
    grows = small // nr
    lots = nc if grows % (GROUP * nc) == 0 else 1
    gcols = grows // lots
    dma = pltpu.SemaphoreType.DMA
    vmem, anywhere = pl.BlockSpec(memory_space=pltpu.VMEM), pl.BlockSpec(memory_space=pl.ANY)
    square = jax.ShapeDtypeStruct((width, width), F32)
    column = jax.ShapeDtypeStruct((kr, width), F32)
    others = max(ratio - 1, 1)
    zlines, glines, clines = eights(kr // GROUP), eights(grows // GROUP), eights(gcols // GROUP)
    I16 = jnp.int16
    summed, small_sums = pl.pallas_call(
        functools.partial(kernel, nr, nc),
        out_shape=(jax.ShapeDtypeStruct((kr, 2 * width), F32), jax.ShapeDtypeStruct((small, BLOCK), F32)),
        in_specs=[anywhere] * 4,
        out_specs=(vmem,) * 2,
        scratch_shapes=[
            pltpu.VMEM(inverse_block.shape, BF16),
            pltpu.VMEM(tile_mask.shape, jnp.int32),
            pltpu.VMEM(factor.shape, BF16),
            pltpu.VMEM(panel_mask.shape, jnp.int32),
            pltpu.VMEM((rows, cols), BF16),
            pltpu.VMEM((rows, 2 * width), BF16),
            pltpu.VMEM((2 * width, rows), BF16),
            pltpu.VMEM((rows, 2 * width), BF16),
            pltpu.VMEM((others, nr, kr, cols), BF16),
            pltpu.VMEM((rows, 2 * width), F32),
            pltpu.VMEM((kr, 2 * width), F32),
            pltpu.VMEM((nr - 1, kr, 2 * width), I16),
            pltpu.VMEM((nr - 1, zlines, 2 * width), F32),
            pltpu.VMEM((nr - 1, kr, 2 * width), I16),
            pltpu.VMEM((nr - 1, zlines, 2 * width), F32),
            pltpu.VMEM((small, BLOCK), F32),
            pltpu.VMEM((small, BLOCK), I16),
            pltpu.VMEM((nr, glines, BLOCK), F32),
            pltpu.VMEM((nr - 1, grows, BLOCK), I16),
            pltpu.VMEM((nr - 1, glines, BLOCK), F32),
            pltpu.VMEM((grows, BLOCK), I16),
            pltpu.VMEM((lots, clines, BLOCK), F32),
            pltpu.VMEM((nc, gcols, BLOCK), I16),
            pltpu.VMEM((nc, clines, BLOCK), F32),
            pltpu.VMEM((small, BLOCK), I16),
            pltpu.VMEM((nr, lots, clines, BLOCK), F32),
            dma((4,)),
            dma((2 * ratio, max(nr // 2, 1))), dma((2 * ratio,)), dma((ratio,)),
            dma((others, nr)), dma((others, nr)),
            dma((2, nr - 1)), dma((2, nr - 1)),
            dma((2, nr - 1)), dma((2, nr - 1)),
            dma((2, nc - 1)), dma((2, nc - 1)),
            dma((2, nc - 1)), dma((2, nc - 1)),
            dma((2, nr - 1)), dma((2, nr - 1)),
        ],
        compiler_params=pltpu.CompilerParams(
            collective_id=0, has_side_effects=True, vmem_limit_bytes=56 * 1024 * 1024
        ),
    )(inverse_block, tile_mask, factor, panel_mask)
    return pl.pallas_call(
        finish,
        out_shape=(column, square, square, column, square),
        in_specs=[vmem] * 4,
        out_specs=(vmem,) * 5,
        compiler_params=pltpu.CompilerParams(vmem_limit_bytes=24 * 1024 * 1024),
    )(summed, small_sums, child_top, pivots)


def solution(mesh):
    in_specs = (P("row", "col"), P("row", "col"), P(None, "row", None), P(None, "row"), P(), P())
    out_specs = (P(("row", "col"), None), P(), P(), P(("row", "col"), None), P())
    body = functools.partial(shards, mesh.shape["row"], mesh.shape["col"])
    return jax.shard_map(body, mesh=mesh, in_specs=in_specs, out_specs=out_specs, check_vma=False)
```

```python
import functools

import jax
import jax.numpy as jnp
from jax import lax
from jax.experimental import pallas as pl
from jax.experimental.pallas import tpu as pltpu
from jax.sharding import PartitionSpec as P

BLOCK = 128
GROUP = 16
MESH = pl.DeviceIdType.MESH
F32 = jnp.float32
BF16 = jnp.bfloat16


def split(a):
    high = a.astype(BF16)
    return high, (a - high.astype(F32)).astype(BF16)


def dot(a, b):
    return jnp.dot(a, b, preferred_element_type=F32)


def dot_t(a, b):
    return lax.dot_general(a, b, (((0,), (0,)), ((), ())), preferred_element_type=F32)


def quantize(a):
    groups = a.shape[0] // GROUP
    parts = a.reshape(groups, GROUP, a.shape[1])
    largest = jnp.maximum(jnp.max(jnp.abs(parts), axis=1), 1e-30)
    whole = jnp.round(parts * (32767.0 / largest)[:, None, :]).astype(jnp.int32)
    return whole.reshape(a.shape).astype(jnp.int16), largest * (1.0 / 32767.0)


def restore(whole, scale):
    groups = whole.shape[0] // GROUP
    parts = whole.astype(jnp.int32).astype(F32).reshape(groups, GROUP, whole.shape[1])
    return (parts * scale[:groups][:, None, :]).reshape(whole.shape)


def kernel(
    nr, nc, m_any, tm_any, f_any, pm_any, sum_ref, g_ref,
    m_ref, tm_ref, f_ref, pm_ref, mk, jown, jt, jz, mx, q, own, zq, zx, zrq, zrx, gp,
    gpq, gps, grq, grs, gtq, gts, gcq, gcs, gfq, gfs, in_sem,
    ps_sem, pr_sem, fs_sem, ms_sem, mr_sem, zs_sem, zr_sem,
    as_sem, ar_sem, bs_sem, br_sem, cs_sem, cr_sem, ds_sem, dr_sem,
):
    r, c = lax.axis_index("row"), lax.axis_index("col")
    ratio = nc // nr
    rows, cols = m_ref.shape
    width = f_ref.shape[2]
    kr = rows // nc
    qr = cols // 2
    grows = gp.shape[0] // nr
    lots = gfs.shape[1]
    shared = lots == 1
    gcols = grows // lots
    x, z = lax.rem(c, ratio), lax.div(c, ratio)
    chip, core = lax.div(r, 2), lax.rem(r, 2)
    chips = nr // 2
    mate = chip * 2 + 1 - core
    is_source = r == z
    same_chip = chip == lax.div(z, 2)
    sent = []

    loads = [
        pltpu.make_async_copy(there, here, in_sem.at[i])
        for i, (there, here) in enumerate(
            ((pm_any, pm_ref), (f_any, f_ref), (tm_any, tm_ref), (m_any, m_ref))
        )
    ]
    for load in loads:
        load.start()

    def copy(src, dst, send, recv, row, col):
        return pltpu.make_async_remote_copy(
            src_ref=src, dst_ref=dst, send_sem=send, recv_sem=recv,
            device_id=(row, col), device_id_type=MESH,
        )

    def start(src, dst, send, recv, row, col):
        made = copy(src, dst, send, recv, row, col)
        made.start()
        sent.append(made)

    def arrived(dst, send, recv):
        copy(dst, dst, send, recv, r, c).wait_recv()

    def at(ref, first, count):
        return ref.at[pl.ds(pl.multiple_of(first, 16), count)]

    barrier = pltpu.get_barrier_semaphore()
    for d in range(1, nr):
        pl.semaphore_signal(
            barrier, inc=1, device_id=(lax.rem(r + d, nr), c), device_id_type=MESH
        )
    for d in range(1, nc):
        pl.semaphore_signal(
            barrier, inc=1, device_id=(r, lax.rem(c + d, nc)), device_id_type=MESH
        )
    loads[0].wait()
    loads[1].wait()
    for b in range(rows // BLOCK):
        part = slice(b * BLOCK, (b + 1) * BLOCK)
        for s in range(2):
            keep = pm_ref[s : s + 1, b : b + 1].astype(F32)
            jown[part, s * width : (s + 1) * width] = (f_ref[s, part, :].astype(F32) * keep).astype(BF16)
    pl.semaphore_wait(barrier, nr + nc - 2)

    def piece(ref, e, h):
        half = lax.rem(x + e, ratio)
        return at(ref, (half * 2 + h) * qr, qr)

    def panel_copies(e):
        made = []
        for h in range(2):
            i = 2 * e + h
            for d in range(1, chips):
                to = lax.rem(chip + d, chips) * 2 + h
                made.append(
                    copy(piece(jown, e, h), piece(jz, e, h), ps_sem.at[i, d], pr_sem.at[i], to, c)
                )
            made.append(
                copy(piece(jown, e, h), piece(jz, e, h), ps_sem.at[i, 0], pr_sem.at[i], mate, c)
            )
        return made

    def forward_copy(e):
        half = lax.rem(x + e, ratio)
        part = at(jz, (half * 2 + core) * qr, qr)
        i = 2 * e + core
        return part, copy(part, part, fs_sem.at[e], pr_sem.at[i], mate, c)

    def panels_arrive(e):
        @pl.when(jnp.logical_and(jnp.logical_not(is_source), same_chip))
        def _():
            for h in range(2):
                arrived(piece(jz, e, h), ps_sem.at[2 * e + h, 0], pr_sem.at[2 * e + h])

        @pl.when(jnp.logical_not(same_chip))
        def _():
            part, made = forward_copy(e)
            arrived(part, fs_sem.at[e], pr_sem.at[2 * e + core])
            made.start()
            half = lax.rem(x + e, ratio)
            other = at(jz, (half * 2 + 1 - core) * qr, qr)
            arrived(other, fs_sem.at[e], pr_sem.at[2 * e + 1 - core])

    @pl.when(is_source)
    def _():
        for made in panel_copies(0):
            made.start()

    loads[2].wait()
    loads[3].wait()
    for b in range(rows // BLOCK):
        for j in range(cols // BLOCK):
            tile = (slice(b * BLOCK, (b + 1) * BLOCK), slice(j * BLOCK, (j + 1) * BLOCK))
            keep = tm_ref[j : j + 1, b : b + 1].astype(F32)
            mk[tile] = (m_ref[tile].astype(F32) * keep).astype(BF16)
    for e in range(nr):
        g = lax.rem(z + 1 + e, nr)
        for d in range(1, ratio):
            xx = lax.rem(x + d, ratio)
            start(
                at(mk, (g * ratio + xx) * kr, kr), mx.at[d - 1, e],
                ms_sem.at[d - 1, e], mr_sem.at[d - 1, e], r, z * ratio + xx,
            )

    jt[...] = jown[...].T

    @pl.when(is_source)
    def _():
        jz[...] = jown[...]
        for made in panel_copies(0):
            made.wait_send()
        for e in range(1, ratio):
            for made in panel_copies(e):
                made.start()

    panels_arrive(0)
    near = jz[pl.ds(pl.multiple_of(x * cols, cols), cols), :]
    step = min(rows, 256)
    for b in range(rows // step):
        part = slice(b * step, (b + 1) * step)
        q[part, :] = dot(mk[part, :], near)

    slots = width // BLOCK
    for s in range(2):
        high, low = split(q[:, s * width : (s + 1) * width])
        turned = jt[s * width :, :]
        value = dot(turned, high) + dot(turned, low)
        for i in range(2 - s):
            for j in range(slots):
                first = ((i + 2 * s) * slots + j) * width
                gp[first : first + width, :] = value[
                    i * width : (i + 1) * width, j * BLOCK : (j + 1) * BLOCK
                ]
    glines = grows // GROUP
    for i in range(nr):
        part = slice(i * grows, (i + 1) * grows)
        gpq[part, :], gps[i, :glines, :] = quantize(gp[part, :])
    for d in range(1, nr):
        to = lax.rem(r + d, nr)
        start(gps.at[to], grs.at[d - 1], as_sem.at[1, d - 1], ar_sem.at[1, d - 1], to, c)
        start(at(gpq, to * grows, grows), grq.at[d - 1], as_sem.at[0, d - 1], ar_sem.at[0, d - 1], to, c)
    for e in range(1, ratio):
        panels_arrive(e)
    zlines = kr // GROUP

    def send_rows(e):
        to = lax.rem(z + 1 + e, nr) * ratio + x
        start(zx.at[e], zrx.at[e], zs_sem.at[1, e], zr_sem.at[1, e], r, to)
        start(zq.at[e], zrq.at[e], zs_sem.at[0, e], zr_sem.at[0, e], r, to)

    for e in range(nr):
        g = lax.rem(z + 1 + e, nr)
        value = q[pl.ds(pl.multiple_of((g * ratio + x) * kr, 16), kr), :]
        for d in range(1, ratio):
            arrived(mx.at[d - 1, e], ms_sem.at[d - 1, e], mr_sem.at[d - 1, e])
            half = lax.rem(x - d + ratio, ratio)
            value = value + dot(mx[d - 1, e], jz[pl.ds(pl.multiple_of(half * cols, cols), cols), :])
        if e < nr - 1:
            zq[e], zx[e, :zlines, :] = quantize(value)
            if e == 0:
                send_rows(e)
        else:
            own[...] = value

    total = gp[pl.ds(pl.multiple_of(r * grows, 16), grows), :]
    for d in range(1, nr):
        arrived(grs.at[d - 1], as_sem.at[1, d - 1], ar_sem.at[1, d - 1])
        arrived(grq.at[d - 1], as_sem.at[0, d - 1], ar_sem.at[0, d - 1])
        total = total + restore(grq[d - 1], grs[d - 1])
    gp[pl.ds(pl.multiple_of(r * grows, 16), grows), :] = total
    lines = gcols // GROUP
    for i in range(lots):
        part = slice(i * gcols, (i + 1) * gcols)
        gtq[part, :], gts[i, :lines, :] = quantize(total[part, :])
    for d in range(1, nc):
        to = lax.rem(c + d, nc)
        place = 0 if shared else to
        start(gts.at[place], gcs.at[c], bs_sem.at[1, d - 1], br_sem.at[1, d - 1], r, to)
        start(at(gtq, place * gcols, gcols), gcq.at[c], bs_sem.at[0, d - 1], br_sem.at[0, d - 1], r, to)
    place = 0 if shared else c
    gcs[pl.ds(c, 1)] = gts[pl.ds(place, 1)]
    gcq[pl.ds(c, 1)] = gtq[pl.ds(pl.multiple_of(place * gcols, 16), gcols), :][None]

    for e in range(1, nr - 1):
        send_rows(e)

    total = None
    for d in range(1, nc):
        come = lax.rem(c + nc - d, nc)
        arrived(gcs.at[come], bs_sem.at[1, d - 1], br_sem.at[1, d - 1])
        arrived(gcq.at[come], bs_sem.at[0, d - 1], br_sem.at[0, d - 1])
    for i in range(nc):
        value = restore(gcq[i], gcs[i])
        total = value if total is None else total + value
    mine = r * grows + place * gcols
    whole, scale = quantize(total)
    gfq[pl.ds(pl.multiple_of(mine, 16), gcols), :] = whole
    padding = gfs.shape[2] - lines
    if padding:
        scale = jnp.concatenate([scale, jnp.zeros((padding, BLOCK), F32)], axis=0)
    gfs[r, place] = scale
    if not shared:
        for d in range(1, nc):
            to = lax.rem(c + d, nc)
            start(gfs.at[r, c], gfs.at[r, c], cs_sem.at[1, d - 1], cr_sem.at[1, d - 1], r, to)
            block = at(gfq, mine, gcols)
            start(block, block, cs_sem.at[0, d - 1], cr_sem.at[0, d - 1], r, to)
        for d in range(1, nc):
            come = lax.rem(c + nc - d, nc)
            arrived(gfs.at[r, come], cs_sem.at[1, d - 1], cr_sem.at[1, d - 1])
            arrived(at(gfq, r * grows + come * gcols, gcols), cs_sem.at[0, d - 1], cr_sem.at[0, d - 1])
    for d in range(1, nr):
        to = lax.rem(r + d, nr)
        start(gfs.at[r], gfs.at[r], ds_sem.at[1, d - 1], dr_sem.at[1, d - 1], to, c)
        block = at(gfq, r * grows, grows)
        start(block, block, ds_sem.at[0, d - 1], dr_sem.at[0, d - 1], to, c)

    value = own[...]
    for e in range(nr - 1):
        arrived(zrx.at[e], zs_sem.at[1, e], zr_sem.at[1, e])
        arrived(zrq.at[e], zs_sem.at[0, e], zr_sem.at[0, e])
        value = value + restore(zrq[e], zrx[e])
    sum_ref[...] = value

    for d in range(1, nr):
        come = lax.rem(r + nr - d, nr)
        arrived(gfs.at[come], ds_sem.at[1, d - 1], dr_sem.at[1, d - 1])
        arrived(at(gfq, come * grows, grows), ds_sem.at[0, d - 1], dr_sem.at[0, d - 1])
    for i in range(nr):
        for j in range(lots):
            part = slice(i * grows + j * gcols, i * grows + (j + 1) * gcols)
            g_ref[part, :] = restore(gfq[part, :], gfs[i, j])

    for made in sent:
        made.wait_send()

    @pl.when(is_source)
    def _():
        for e in range(1, ratio):
            for made in panel_copies(e):
                made.wait_send()

    @pl.when(jnp.logical_not(same_chip))
    def _():
        for e in range(ratio):
            forward_copy(e)[1].wait_send()


def finish(sum_ref, g_ref, top_ref, piv_ref, pc_ref, pd_ref, cu_ref, cc_ref, cd_ref):
    width = top_ref.shape[0]
    slots = width // BLOCK
    top = top_ref[...]
    value = sum_ref[...]
    parent = value[:, :width]
    high, low = split(parent)
    pc_ref[...] = -parent
    cc_ref[...] = dot(high, top) + dot(low, top) - value[:, width:]

    def square(i):
        return jnp.concatenate(
            [g_ref[(i * slots + j) * width : (i * slots + j + 1) * width, :] for j in range(slots)], axis=1
        )

    diag = piv_ref[0] + square(0)
    pd_ref[...] = diag
    cross = square(1)
    high, low = split(diag)
    upper = cross.T - (dot(high, top) + dot(low, top))
    cu_ref[...] = upper
    high, low = split(upper)
    cross_high, cross_low = split(cross)
    cd_ref[...] = (
        piv_ref[1] - (dot_t(top, high) + dot_t(top, low))
        - (dot(cross_high, top) + dot(cross_low, top)) + square(2)
    )


def eights(count):
    return -(-count // 8) * 8


def shards(nr, nc, inverse_block, tile_mask, factor, panel_mask, child_top, pivots):
    rows, cols = inverse_block.shape
    width = factor.shape[2]
    ratio = nc // nr
    kr = rows // nc
    small = 3 * width * width // BLOCK
    grows = small // nr
    lots = nc if grows % (GROUP * nc) == 0 else 1
    gcols = grows // lots
    dma = pltpu.SemaphoreType.DMA
    vmem, anywhere = pl.BlockSpec(memory_space=pltpu.VMEM), pl.BlockSpec(memory_space=pl.ANY)
    square = jax.ShapeDtypeStruct((width, width), F32)
    column = jax.ShapeDtypeStruct((kr, width), F32)
    others = max(ratio - 1, 1)
    zlines, glines, clines = eights(kr // GROUP), eights(grows // GROUP), eights(gcols // GROUP)
    I16 = jnp.int16
    summed, small_sums = pl.pallas_call(
        functools.partial(kernel, nr, nc),
        out_shape=(pltpu.VMEM((kr, 2 * width), F32), pltpu.VMEM((small, BLOCK), F32)),
        in_specs=[anywhere] * 4,
        out_specs=(vmem,) * 2,
        scratch_shapes=[
            pltpu.VMEM(inverse_block.shape, BF16),
            pltpu.VMEM(tile_mask.shape[::-1], jnp.int32),
            pltpu.VMEM(factor.shape, BF16),
            pltpu.VMEM(panel_mask.shape, jnp.int32),
            pltpu.VMEM((rows, cols), BF16),
            pltpu.VMEM((rows, 2 * width), BF16),
            pltpu.VMEM((2 * width, rows), BF16),
            pltpu.VMEM((rows, 2 * width), BF16),
            pltpu.VMEM((others, nr, kr, cols), BF16),
            pltpu.VMEM((rows, 2 * width), F32),
            pltpu.VMEM((kr, 2 * width), F32),
            pltpu.VMEM((nr - 1, kr, 2 * width), I16),
            pltpu.VMEM((nr - 1, zlines, 2 * width), F32),
            pltpu.VMEM((nr - 1, kr, 2 * width), I16),
            pltpu.VMEM((nr - 1, zlines, 2 * width), F32),
            pltpu.VMEM((small, BLOCK), F32),
            pltpu.VMEM((small, BLOCK), I16),
            pltpu.VMEM((nr, glines, BLOCK), F32),
            pltpu.VMEM((nr - 1, grows, BLOCK), I16),
            pltpu.VMEM((nr - 1, glines, BLOCK), F32),
            pltpu.VMEM((grows, BLOCK), I16),
            pltpu.VMEM((lots, clines, BLOCK), F32),
            pltpu.VMEM((nc, gcols, BLOCK), I16),
            pltpu.VMEM((nc, clines, BLOCK), F32),
            pltpu.VMEM((small, BLOCK), I16),
            pltpu.VMEM((nr, lots, clines, BLOCK), F32),
            dma((4,)),
            dma((2 * ratio, max(nr // 2, 1))), dma((2 * ratio,)), dma((ratio,)),
            dma((others, nr)), dma((others, nr)),
            dma((2, nr - 1)), dma((2, nr - 1)),
            dma((2, nr - 1)), dma((2, nr - 1)),
            dma((2, nc - 1)), dma((2, nc - 1)),
            dma((2, nc - 1)), dma((2, nc - 1)),
            dma((2, nr - 1)), dma((2, nr - 1)),
        ],
        compiler_params=pltpu.CompilerParams(
            collective_id=0, has_side_effects=True, vmem_limit_bytes=56 * 1024 * 1024
        ),
    )(inverse_block, tile_mask.T, factor, panel_mask)
    return pl.pallas_call(
        finish,
        out_shape=(column, square, square, column, square),
        in_specs=[vmem] * 4,
        out_specs=(vmem,) * 5,
        compiler_params=pltpu.CompilerParams(vmem_limit_bytes=24 * 1024 * 1024),
    )(summed, small_sums, child_top, pivots)


def solution(mesh):
    in_specs = (P("row", "col"), P("row", "col"), P(None, "row", None), P(None, "row"), P(), P())
    out_specs = (P(("row", "col"), None), P(), P(), P(("row", "col"), None), P())
    body = functools.partial(shards, mesh.shape["row"], mesh.shape["col"])
    return jax.shard_map(body, mesh=mesh, in_specs=in_specs, out_specs=out_specs, check_vma=False)
```

```python
import functools

import jax
import jax.numpy as jnp
from jax import lax
from jax.experimental import pallas as pl
from jax.experimental.pallas import tpu as pltpu
from jax.sharding import PartitionSpec as P

BLOCK = 128
GROUP = 16
MESH = pl.DeviceIdType.MESH
F32 = jnp.float32
BF16 = jnp.bfloat16


def split(a):
    high = a.astype(BF16)
    return high, (a - high.astype(F32)).astype(BF16)


def dot(a, b):
    return jnp.dot(a, b, preferred_element_type=F32)


def dot_t(a, b):
    return lax.dot_general(a, b, (((0,), (0,)), ((), ())), preferred_element_type=F32)


def packed(rows):
    return rows + -(-(rows // GROUP) // GROUP) * GROUP


def pack(a):
    groups = a.shape[0] // GROUP
    parts = a.reshape(groups, GROUP, a.shape[1])
    largest = jnp.maximum(jnp.max(jnp.abs(parts), axis=1), 1e-30)
    power = jnp.ceil(jnp.log2(largest) - 14.99)
    whole = jnp.round(parts * jnp.exp2(-power)[:, None, :]).astype(jnp.int32)
    whole = whole.reshape(a.shape).astype(jnp.int16)
    padding = packed(a.shape[0]) - a.shape[0] - groups
    if padding:
        power = jnp.concatenate([power, jnp.zeros((padding, a.shape[1]), F32)], axis=0)
    return jnp.concatenate([whole, power.astype(jnp.int32).astype(jnp.int16)], axis=0)


def unpack(held, rows):
    groups = rows // GROUP
    scale = jnp.exp2(held[rows:].astype(jnp.int32).astype(F32))[:groups]
    parts = held[:rows].astype(jnp.int32).astype(F32).reshape(groups, GROUP, held.shape[1])
    return (parts * scale[:, None, :]).reshape(rows, held.shape[1])


def kernel(
    nr, nc, lots, m_any, tm_any, f_any, pm_any, sum_ref, g_ref,
    m_ref, tm_ref, f_ref, pm_ref, mk, jown, jt, jz, mx, q, zq, zrq,
    hf, h1, h1r, h2, h2r, gt, gc, gf, in_sem,
    ps_sem, pr_sem, fs_sem, ms_sem, mr_sem, zs_sem, zr_sem,
    as_sem, ar_sem, es_sem, er_sem, bs_sem, br_sem, cs_sem, cr_sem, ds_sem, dr_sem, xs_sem, xr_sem,
):
    r, c = lax.axis_index("row"), lax.axis_index("col")
    ratio = nc // nr
    rows, cols = m_ref.shape
    width = f_ref.shape[2]
    kr = rows // nc
    qr = cols // 2
    grows = g_ref.shape[0] // nr
    shared = lots == 1
    gcols = grows // lots
    share = width // nr
    hrows = 2 * share
    x, z = lax.rem(c, ratio), lax.div(c, ratio)
    chip, core = lax.div(r, 2), lax.rem(r, 2)
    chips = nr // 2
    mate = chip * 2 + 1 - core
    is_source = r == z
    same_chip = chip == lax.div(z, 2)
    sent = []

    loads = [
        pltpu.make_async_copy(there, here, in_sem.at[i])
        for i, (there, here) in enumerate(
            ((pm_any, pm_ref), (f_any, f_ref), (tm_any, tm_ref), (m_any, m_ref))
        )
    ]
    for load in loads:
        load.start()

    def copy(src, dst, send, recv, row, col):
        return pltpu.make_async_remote_copy(
            src_ref=src, dst_ref=dst, send_sem=send, recv_sem=recv,
            device_id=(row, col), device_id_type=MESH,
        )

    def start(src, dst, send, recv, row, col):
        made = copy(src, dst, send, recv, row, col)
        made.start()
        sent.append(made)

    def arrived(dst, send, recv):
        copy(dst, dst, send, recv, r, c).wait_recv()

    def at(ref, first, count):
        return ref.at[pl.ds(pl.multiple_of(first, 16), count)]

    barrier = pltpu.get_barrier_semaphore()
    for d in range(1, nr):
        pl.semaphore_signal(
            barrier, inc=1, device_id=(lax.rem(r + d, nr), c), device_id_type=MESH
        )
    for d in range(1, nc):
        pl.semaphore_signal(
            barrier, inc=1, device_id=(r, lax.rem(c + d, nc)), device_id_type=MESH
        )
    loads[0].wait()
    loads[1].wait()
    for b in range(rows // BLOCK):
        part = slice(b * BLOCK, (b + 1) * BLOCK)
        for s in range(2):
            keep = pm_ref[s : s + 1, b : b + 1].astype(F32)
            jown[part, s * width : (s + 1) * width] = (f_ref[s, part, :].astype(F32) * keep).astype(BF16)
    pl.semaphore_wait(barrier, nr + nc - 2)

    def piece(ref, e, h):
        half = lax.rem(x + e, ratio)
        return at(ref, (half * 2 + h) * qr, qr)

    def panel_copies(e):
        made = []
        for h in range(2):
            i = 2 * e + h
            for d in range(1, chips):
                to = lax.rem(chip + d, chips) * 2 + h
                made.append(
                    copy(piece(jown, e, h), piece(jz, e, h), ps_sem.at[i, d], pr_sem.at[i], to, c)
                )
            made.append(
                copy(piece(jown, e, h), piece(jz, e, h), ps_sem.at[i, 0], pr_sem.at[i], mate, c)
            )
        return made

    def forward_copy(e):
        half = lax.rem(x + e, ratio)
        part = at(jz, (half * 2 + core) * qr, qr)
        i = 2 * e + core
        return part, copy(part, part, fs_sem.at[e], pr_sem.at[i], mate, c)

    def panels_arrive(e):
        @pl.when(jnp.logical_and(jnp.logical_not(is_source), same_chip))
        def _():
            for h in range(2):
                arrived(piece(jz, e, h), ps_sem.at[2 * e + h, 0], pr_sem.at[2 * e + h])

        @pl.when(jnp.logical_not(same_chip))
        def _():
            part, made = forward_copy(e)
            arrived(part, fs_sem.at[e], pr_sem.at[2 * e + core])
            made.start()
            half = lax.rem(x + e, ratio)
            other = at(jz, (half * 2 + 1 - core) * qr, qr)
            arrived(other, fs_sem.at[e], pr_sem.at[2 * e + 1 - core])

    @pl.when(is_source)
    def _():
        for made in panel_copies(0):
            made.start()

    loads[2].wait()
    loads[3].wait()
    for b in range(rows // BLOCK):
        for j in range(cols // BLOCK):
            tile = (slice(b * BLOCK, (b + 1) * BLOCK), slice(j * BLOCK, (j + 1) * BLOCK))
            keep = tm_ref[j : j + 1, b : b + 1].astype(F32)
            mk[tile] = (m_ref[tile].astype(F32) * keep).astype(BF16)
    for e in range(nr):
        g = lax.rem(z + 1 + e, nr)
        for d in range(1, ratio):
            xx = lax.rem(x + d, ratio)
            start(
                at(mk, (g * ratio + xx) * kr, kr), mx.at[d - 1, e],
                ms_sem.at[d - 1, e], mr_sem.at[d - 1, e], r, z * ratio + xx,
            )

    jt[...] = jown[...].T
    for i in range(2):
        for k in range(2 * width // 256):
            part = slice(k * 256, (k + 1) * 256)
            half = slice(i * cols // 2, (i + 1) * cols // 2)
            hf[part, half] = dot(jt[part, :], mk[:, half])

    def chunk(to):
        first = pl.multiple_of(to * share, 16)
        return jnp.concatenate([hf[pl.ds(first, share), :], hf[pl.ds(width + first, share), :]], axis=0)

    for i in range(chips):
        h1[i] = pack(chunk(i * 2 + 1 - core))
    start(h1, h1r, as_sem.at[0], ar_sem.at[0], mate, c)
    arrived(h1r, as_sem.at[0], ar_sem.at[0])
    for d in range(1, chips):
        there = lax.rem(chip + d, chips)
        h2[d - 1] = pack(chunk(there * 2 + core) + unpack(h1r[there], hrows))
        start(h2.at[d - 1], h2r.at[d - 1], es_sem.at[d - 1], er_sem.at[d - 1], there * 2 + core, c)

    @pl.when(is_source)
    def _():
        jz[...] = jown[...]
        for made in panel_copies(0):
            made.wait_send()
        for e in range(1, ratio):
            for made in panel_copies(e):
                made.start()

    total = chunk(r) + unpack(h1r[chip], hrows)

    panels_arrive(0)
    near = jz[pl.ds(pl.multiple_of(x * cols, cols), cols), :]
    for e in range(nr):
        g = lax.rem(z + 1 + e, nr)
        q[e] = dot(mk[pl.ds(pl.multiple_of((g * ratio + x) * kr, 16), kr), :], near)

    for d in range(1, chips):
        arrived(h2r.at[d - 1], es_sem.at[d - 1], er_sem.at[d - 1])
        total = total + unpack(h2r[d - 1], hrows)
    high, low = split(total)
    parent = dot(high[:share], near[:, :width]) + dot(low[:share], near[:, :width])
    both = dot(high[share:], near) + dot(low[share:], near)
    slots = width // BLOCK
    pieces = [parent[:, j * BLOCK : (j + 1) * BLOCK] for j in range(slots)]
    pieces += [both[:, j * BLOCK : (j + 1) * BLOCK] for j in range(2 * slots)]
    total = jnp.concatenate(pieces, axis=0)

    for i in range(lots):
        gt[i] = pack(total[i * gcols : (i + 1) * gcols, :])
    for d in range(1, nc):
        to = lax.rem(c + d, nc)
        start(gt.at[0 if shared else to], gc.at[c], bs_sem.at[d - 1], br_sem.at[d - 1], r, to)
    place = 0 if shared else c
    gc[pl.ds(c, 1)] = gt[pl.ds(place, 1)]

    for e in range(1, ratio):
        panels_arrive(e)
    for e in range(nr):
        value = q[e]
        for d in range(1, ratio):
            arrived(mx.at[d - 1, e], ms_sem.at[d - 1, e], mr_sem.at[d - 1, e])
            half = lax.rem(x - d + ratio, ratio)
            value = value + dot(mx[d - 1, e], jz[pl.ds(pl.multiple_of(half * cols, cols), cols), :])
        if e < nr - 1:
            zq[e] = pack(value)
            to = lax.rem(z + 1 + e, nr) * ratio + x
            start(zq.at[e], zrq.at[e], zs_sem.at[e], zr_sem.at[e], r, to)
        else:
            q[e] = value

    for d in range(1, nc):
        come = lax.rem(c + nc - d, nc)
        arrived(gc.at[come], bs_sem.at[d - 1], br_sem.at[d - 1])
    total = unpack(gc[0], gcols)
    for i in range(1, nc):
        total = total + unpack(gc[i], gcols)
    gf[r, place] = pack(total)
    if not shared:
        for d in range(1, nc):
            to = lax.rem(c + d, nc)
            start(gf.at[r, c], gf.at[r, c], cs_sem.at[d - 1], cr_sem.at[d - 1], r, to)
        for d in range(1, nc):
            come = lax.rem(c + nc - d, nc)
            arrived(gf.at[r, come], cs_sem.at[d - 1], cr_sem.at[d - 1])
    for d in range(1, chips):
        to = lax.rem(chip + d, chips) * 2 + core
        start(gf.at[r], gf.at[r], ds_sem.at[d - 1], dr_sem.at[d - 1], to, c)
    start(gf.at[r], gf.at[r], xs_sem.at[0], xr_sem.at[0], mate, c)
    for d in range(1, chips):
        come = lax.rem(chip + chips - d, chips) * 2 + core
        arrived(gf.at[come], ds_sem.at[d - 1], dr_sem.at[d - 1])
        start(gf.at[come], gf.at[come], xs_sem.at[d], xr_sem.at[d], mate, c)

    value = q[nr - 1]
    for e in range(nr - 1):
        arrived(zrq.at[e], zs_sem.at[e], zr_sem.at[e])
        value = value + unpack(zrq[e], kr)
    sum_ref[...] = value

    for d in range(chips):
        come = lax.rem(chip + chips - d, chips) * 2 + 1 - core
        arrived(gf.at[come], xs_sem.at[d], xr_sem.at[d])
    for i in range(nr):
        block = jnp.concatenate([unpack(gf[i, j], gcols) for j in range(lots)], axis=0)
        for k in range(3 * slots):
            g_ref[k * width + i * share : k * width + (i + 1) * share, :] = block[k * share : (k + 1) * share, :]

    for made in sent:
        made.wait_send()

    @pl.when(is_source)
    def _():
        for e in range(1, ratio):
            for made in panel_copies(e):
                made.wait_send()

    @pl.when(jnp.logical_not(same_chip))
    def _():
        for e in range(ratio):
            forward_copy(e)[1].wait_send()


def finish(sum_ref, g_ref, top_ref, piv_ref, pc_ref, pd_ref, cu_ref, cc_ref, cd_ref):
    width = top_ref.shape[0]
    slots = width // BLOCK
    top = top_ref[...]
    value = sum_ref[...]
    parent = value[:, :width]
    high, low = split(parent)
    pc_ref[...] = -parent
    cc_ref[...] = dot(high, top) + dot(low, top) - value[:, width:]

    def square(i):
        return jnp.concatenate(
            [g_ref[(i * slots + j) * width : (i * slots + j + 1) * width, :] for j in range(slots)], axis=1
        )

    diag = piv_ref[0] + square(0)
    pd_ref[...] = diag
    cross = square(1)
    high, low = split(diag)
    upper = cross.T - (dot(high, top) + dot(low, top))
    cu_ref[...] = upper
    high, low = split(upper)
    cross_high, cross_low = split(cross)
    cd_ref[...] = (
        piv_ref[1] - (dot_t(top, high) + dot_t(top, low))
        - (dot(cross_high, top) + dot(cross_low, top)) + square(2)
    )


def shards(nr, nc, inverse_block, tile_mask, factor, panel_mask, child_top, pivots):
    rows, cols = inverse_block.shape
    width = factor.shape[2]
    ratio = nc // nr
    kr = rows // nc
    small = 3 * width * width // BLOCK
    grows = small // nr
    lots = nc if grows % (GROUP * nc) == 0 else 1
    gcols = grows // lots
    dma = pltpu.SemaphoreType.DMA
    vmem, anywhere = pl.BlockSpec(memory_space=pltpu.VMEM), pl.BlockSpec(memory_space=pl.ANY)
    square = jax.ShapeDtypeStruct((width, width), F32)
    column = jax.ShapeDtypeStruct((kr, width), F32)
    others = max(ratio - 1, 1)
    chips, hrows = nr // 2, 2 * width // nr
    I16 = jnp.int16
    summed, small_sums = pl.pallas_call(
        functools.partial(kernel, nr, nc, lots),
        out_shape=(pltpu.VMEM((kr, 2 * width), F32), pltpu.VMEM((small, BLOCK), F32)),
        in_specs=[anywhere] * 4,
        out_specs=(vmem,) * 2,
        scratch_shapes=[
            pltpu.VMEM(inverse_block.shape, BF16),
            pltpu.VMEM(tile_mask.shape[::-1], jnp.int32),
            pltpu.VMEM(factor.shape, BF16),
            pltpu.VMEM(panel_mask.shape, jnp.int32),
            pltpu.VMEM((rows, cols), BF16),
            pltpu.VMEM((rows, 2 * width), BF16),
            pltpu.VMEM((2 * width, rows), BF16),
            pltpu.VMEM((rows, 2 * width), BF16),
            pltpu.VMEM((others, nr, kr, cols), BF16),
            pltpu.VMEM((nr, kr, 2 * width), F32),
            pltpu.VMEM((nr - 1, packed(kr), 2 * width), I16),
            pltpu.VMEM((nr - 1, packed(kr), 2 * width), I16),
            pltpu.VMEM((2 * width, cols), F32),
            pltpu.VMEM((chips, packed(hrows), cols), I16),
            pltpu.VMEM((chips, packed(hrows), cols), I16),
            pltpu.VMEM((chips - 1, packed(hrows), cols), I16),
            pltpu.VMEM((chips - 1, packed(hrows), cols), I16),
            pltpu.VMEM((lots, packed(gcols), BLOCK), I16),
            pltpu.VMEM((nc, packed(gcols), BLOCK), I16),
            pltpu.VMEM((nr, lots, packed(gcols), BLOCK), I16),
            dma((4,)),
            dma((2 * ratio, max(nr // 2, 1))), dma((2 * ratio,)), dma((ratio,)),
            dma((others, nr)), dma((others, nr)),
            dma((nr - 1,)), dma((nr - 1,)),
            dma((1,)), dma((1,)), dma((chips - 1,)), dma((chips - 1,)),
            dma((nc - 1,)), dma((nc - 1,)), dma((nc - 1,)), dma((nc - 1,)),
            dma((chips - 1,)), dma((chips - 1,)), dma((chips,)), dma((chips,)),
        ],
        compiler_params=pltpu.CompilerParams(
            collective_id=0, has_side_effects=True, vmem_limit_bytes=56 * 1024 * 1024
        ),
    )(inverse_block, tile_mask.T, factor, panel_mask)
    return pl.pallas_call(
        finish,
        out_shape=(column, square, square, column, square),
        in_specs=[vmem] * 4,
        out_specs=(vmem,) * 5,
        compiler_params=pltpu.CompilerParams(vmem_limit_bytes=24 * 1024 * 1024),
    )(summed, small_sums, child_top, pivots)


def solution(mesh):
    in_specs = (P("row", "col"), P("row", "col"), P(None, "row", None), P(None, "row"), P(), P())
    out_specs = (P(("row", "col"), None), P(), P(), P(("row", "col"), None), P())
    body = functools.partial(shards, mesh.shape["row"], mesh.shape["col"])
    return jax.shard_map(body, mesh=mesh, in_specs=in_specs, out_specs=out_specs, check_vma=False)
```

```python
import functools

import jax
import jax.numpy as jnp
from jax import lax
from jax.experimental import pallas as pl
from jax.experimental.pallas import tpu as pltpu
from jax.sharding import PartitionSpec as P

BLOCK = 128
GROUP = 16
WIDE = 32
MESH = pl.DeviceIdType.MESH
F32 = jnp.float32
BF16 = jnp.bfloat16


def split(a):
    high = a.astype(BF16)
    return high, (a - high.astype(F32)).astype(BF16)


def dot(a, b):
    return jnp.dot(a, b, preferred_element_type=F32)


def dot_t(a, b):
    return lax.dot_general(a, b, (((0,), (0,)), ((), ())), preferred_element_type=F32)


def packed(rows, group=GROUP):
    return rows + -(-(rows // group) // 16) * 16


def pack(a, group=GROUP):
    groups = a.shape[0] // group
    parts = a.reshape(groups, group, a.shape[1])
    largest = jnp.maximum(jnp.max(jnp.abs(parts), axis=1), 1e-30)
    power = jnp.ceil(jnp.log2(largest) - 14.99)
    whole = jnp.round(parts * jnp.exp2(-power)[:, None, :]).astype(jnp.int32)
    whole = whole.reshape(a.shape).astype(jnp.int16)
    padding = packed(a.shape[0], group) - a.shape[0] - groups
    if padding:
        power = jnp.concatenate([power, jnp.zeros((padding, a.shape[1]), F32)], axis=0)
    return jnp.concatenate([whole, power.astype(jnp.int32).astype(jnp.int16)], axis=0)


def unpack(held, rows, group=GROUP):
    groups = rows // group
    scale = jnp.exp2(held[rows:].astype(jnp.int32).astype(F32))[:groups]
    parts = held[:rows].astype(jnp.int32).astype(F32).reshape(groups, group, held.shape[1])
    return (parts * scale[:, None, :]).reshape(rows, held.shape[1])


def fold(a):
    return jnp.concatenate([a[:, j : j + BLOCK] for j in range(0, a.shape[1], BLOCK)], axis=0)


def unfold(a, rows):
    return jnp.concatenate([a[i : i + rows] for i in range(0, a.shape[0], rows)], axis=1)


def kernel(
    nr, nc, lots, m_any, tm_any, f_any, pm_any, sum_ref, g_ref,
    m_ref, tm_ref, f_ref, pm_ref, mk, jown, jt, jz, mx, q, zq, zrq,
    hf, h1, h1r, h2, h2r, gt, gc, gf, in_sem,
    ps_sem, pr_sem, fs_sem, ms_sem, mr_sem, zs_sem, zr_sem,
    as_sem, ar_sem, es_sem, er_sem, bs_sem, br_sem, cs_sem, cr_sem, ds_sem, dr_sem, xs_sem, xr_sem,
):
    r, c = lax.axis_index("row"), lax.axis_index("col")
    ratio = nc // nr
    rows, cols = m_ref.shape
    x, z = lax.rem(c, ratio), lax.div(c, ratio)
    width = f_ref.shape[2]
    kr = rows // nc
    qr = cols // 2
    grows = g_ref.shape[0] // nr
    shared = lots == 1
    gcols = grows // lots
    share = width // nr
    hrows = 2 * share
    hlong = hrows * cols // BLOCK
    zlong = kr * 2 * width // BLOCK
    half = nr // 2
    pair, side = lax.div(z, 2), lax.rem(z, 2)

    def pair_dest(m, which):
        return lax.rem(pair + m, half) * 2 + which

    order = [pair_dest(m, 1 - side) for m in range(1, half)]
    order += [pair_dest(m, side) for m in range(1, half)]
    order += [pair_dest(0, 1 - side), z]
    chip, core = lax.div(r, 2), lax.rem(r, 2)
    chips = nr // 2
    mate = chip * 2 + 1 - core
    is_source = r == z
    same_chip = chip == lax.div(z, 2)
    sent = []

    loads = [
        pltpu.make_async_copy(there, here, in_sem.at[i])
        for i, (there, here) in enumerate(
            ((pm_any, pm_ref), (f_any, f_ref), (tm_any, tm_ref), (m_any, m_ref))
        )
    ]
    for load in loads:
        load.start()

    def copy(src, dst, send, recv, row, col):
        return pltpu.make_async_remote_copy(
            src_ref=src, dst_ref=dst, send_sem=send, recv_sem=recv,
            device_id=(row, col), device_id_type=MESH,
        )

    def start(src, dst, send, recv, row, col):
        made = copy(src, dst, send, recv, row, col)
        made.start()
        sent.append(made)

    def arrived(dst, send, recv):
        copy(dst, dst, send, recv, r, c).wait_recv()

    def at(ref, first, count):
        return ref.at[pl.ds(pl.multiple_of(first, 16), count)]

    barrier = pltpu.get_barrier_semaphore()
    for d in range(1, nr):
        pl.semaphore_signal(
            barrier, inc=1, device_id=(lax.rem(r + d, nr), c), device_id_type=MESH
        )
    for d in range(1, nc):
        pl.semaphore_signal(
            barrier, inc=1, device_id=(r, lax.rem(c + d, nc)), device_id_type=MESH
        )
    loads[0].wait()
    loads[1].wait()
    for b in range(rows // BLOCK):
        part = slice(b * BLOCK, (b + 1) * BLOCK)
        for s in range(2):
            keep = pm_ref[s : s + 1, b : b + 1].astype(F32)
            jown[part, s * width : (s + 1) * width] = (f_ref[s, part, :].astype(F32) * keep).astype(BF16)
    pl.semaphore_wait(barrier, nr + nc - 2)

    def piece(ref, e, h):
        part_of = lax.rem(x + e, ratio)
        return at(ref, (part_of * 2 + h) * qr, qr)

    def panel_copies(e):
        made = []
        for h in range(2):
            i = 2 * e + h
            for d in range(1, chips):
                to = lax.rem(chip + d, chips) * 2 + h
                made.append(
                    copy(piece(jown, e, h), piece(jz, e, h), ps_sem.at[i, d], pr_sem.at[i], to, c)
                )
            made.append(
                copy(piece(jown, e, h), piece(jz, e, h), ps_sem.at[i, 0], pr_sem.at[i], mate, c)
            )
        return made

    def forward_copy(e):
        part_of = lax.rem(x + e, ratio)
        part = at(jz, (part_of * 2 + core) * qr, qr)
        i = 2 * e + core
        return part, copy(part, part, fs_sem.at[e], pr_sem.at[i], mate, c)

    def panels_forward(e):
        @pl.when(jnp.logical_not(same_chip))
        def _():
            part, made = forward_copy(e)
            arrived(part, fs_sem.at[e], pr_sem.at[2 * e + core])
            made.start()

    def panels_arrive(e):
        @pl.when(jnp.logical_and(jnp.logical_not(is_source), same_chip))
        def _():
            for h in range(2):
                arrived(piece(jz, e, h), ps_sem.at[2 * e + h, 0], pr_sem.at[2 * e + h])

        @pl.when(jnp.logical_not(same_chip))
        def _():
            other = at(jz, (lax.rem(x + e, ratio) * 2 + 1 - core) * qr, qr)
            arrived(other, fs_sem.at[e], pr_sem.at[2 * e + 1 - core])

    @pl.when(is_source)
    def _():
        for made in panel_copies(0):
            made.start()

    loads[2].wait()
    loads[3].wait()
    for b in range(rows // BLOCK):
        for j in range(cols // BLOCK):
            tile = (slice(b * BLOCK, (b + 1) * BLOCK), slice(j * BLOCK, (j + 1) * BLOCK))
            keep = tm_ref[j : j + 1, b : b + 1].astype(F32)
            mk[tile] = (m_ref[tile].astype(F32) * keep).astype(BF16)
    for e, g in enumerate(order):
        for d in range(1, ratio):
            xx = lax.rem(x + d, ratio)
            start(
                at(mk, (g * ratio + xx) * kr, kr), mx.at[d - 1, e],
                ms_sem.at[d - 1, e], mr_sem.at[d - 1, e], r, z * ratio + xx,
            )

    jt[...] = jown[...].T
    for i in range(2):
        for k in range(2 * width // 256):
            part = slice(k * 256, (k + 1) * 256)
            span = slice(i * cols // 2, (i + 1) * cols // 2)
            hf[part, span] = dot(jt[part, :], mk[:, span])

    def chunk(to):
        first = pl.multiple_of(to * share, 16)
        return fold(jnp.concatenate([hf[pl.ds(first, share), :], hf[pl.ds(width + first, share), :]], axis=0))

    for i in range(chips):
        h1[i] = pack(chunk(i * 2 + 1 - core), WIDE)
    start(h1, h1r, as_sem.at[0], ar_sem.at[0], mate, c)
    arrived(h1r, as_sem.at[0], ar_sem.at[0])
    for d in range(1, chips):
        there = lax.rem(chip + d, chips)
        h2[d - 1] = pack(chunk(there * 2 + core) + unpack(h1r[there], hlong, WIDE), WIDE)
        start(h2.at[d - 1], h2r.at[d - 1], es_sem.at[d - 1], er_sem.at[d - 1], there * 2 + core, c)

    @pl.when(is_source)
    def _():
        jz[...] = jown[...]
        for made in panel_copies(0):
            made.wait_send()
        for e in range(1, ratio):
            for made in panel_copies(e):
                made.start()

    total = chunk(r) + unpack(h1r[chip], hlong, WIDE)

    panels_forward(0)
    panels_arrive(0)
    near = jz[pl.ds(pl.multiple_of(x * cols, cols), cols), :]
    for e, g in enumerate(order):
        q[e] = dot(mk[pl.ds(pl.multiple_of((g * ratio + x) * kr, 16), kr), :], near)

    for d in range(1, chips):
        arrived(h2r.at[d - 1], es_sem.at[d - 1], er_sem.at[d - 1])
        total = total + unpack(h2r[d - 1], hlong, WIDE)
    total = unfold(total, hrows)
    high, low = split(total)
    parent = dot(high[:share], near[:, :width]) + dot(low[:share], near[:, :width])
    both = dot(high[share:], near) + dot(low[share:], near)
    slots = width // BLOCK
    pieces = [parent[:, j * BLOCK : (j + 1) * BLOCK] for j in range(slots)]
    pieces += [both[:, j * BLOCK : (j + 1) * BLOCK] for j in range(2 * slots)]
    total = jnp.concatenate(pieces, axis=0)

    for i in range(lots):
        gt[i] = pack(total[i * gcols : (i + 1) * gcols, :])
    for d in range(1, nc):
        to = lax.rem(c + d, nc)
        start(gt.at[0 if shared else to], gc.at[c], bs_sem.at[d - 1], br_sem.at[d - 1], r, to)
    place = 0 if shared else c
    gc[pl.ds(c, 1)] = gt[pl.ds(place, 1)]

    for e in range(1, ratio):
        panels_forward(e)
    for d in range(1, nc):
        come = lax.rem(c + nc - d, nc)
        arrived(gc.at[come], bs_sem.at[d - 1], br_sem.at[d - 1])
    total = unpack(gc[0], gcols)
    for i in range(1, nc):
        total = total + unpack(gc[i], gcols)
    gf[r, place] = pack(total)
    if not shared:
        for d in range(1, nc):
            to = lax.rem(c + d, nc)
            start(gf.at[r, c], gf.at[r, c], cs_sem.at[d - 1], cr_sem.at[d - 1], r, to)

    for e in range(1, ratio):
        panels_arrive(e)

    def send_rows(value, i, to):
        zq[i] = pack(value, WIDE)
        start(zq.at[i], zrq.at[i], zs_sem.at[i], zr_sem.at[i], r, to * ratio + x)

    for e in range(nr):
        value = q[e]
        for d in range(1, ratio):
            arrived(mx.at[d - 1, e], ms_sem.at[d - 1, e], mr_sem.at[d - 1, e])
            other = lax.rem(x - d + ratio, ratio)
            value = value + dot(mx[d - 1, e], jz[pl.ds(pl.multiple_of(other * cols, cols), cols), :])
        if e < half - 1:
            send_rows(fold(value), e, pair_dest(0, 1 - side))
        elif e == nr - 2:
            send_rows(fold(value), half - 1, pair_dest(0, 1 - side))
        else:
            q[e] = value
    for m in range(1, half):
        arrived(zrq.at[m - 1], zs_sem.at[m - 1], zr_sem.at[m - 1])
        value = fold(q[half + m - 2]) + unpack(zrq[m - 1], zlong, WIDE)
        send_rows(value, half + m - 1, pair_dest(m, side))

    if not shared:
        for d in range(1, nc):
            come = lax.rem(c + nc - d, nc)
            arrived(gf.at[r, come], cs_sem.at[d - 1], cr_sem.at[d - 1])
    for d in range(1, chips):
        to = lax.rem(chip + d, chips) * 2 + core
        start(gf.at[r], gf.at[r], ds_sem.at[d - 1], dr_sem.at[d - 1], to, c)
    start(gf.at[r], gf.at[r], xs_sem.at[0], xr_sem.at[0], mate, c)
    for d in range(1, chips):
        come = lax.rem(chip + chips - d, chips) * 2 + core
        arrived(gf.at[come], ds_sem.at[d - 1], dr_sem.at[d - 1])
        start(gf.at[come], gf.at[come], xs_sem.at[d], xr_sem.at[d], mate, c)

    value = fold(q[nr - 1])
    for i in range(half - 1, nr - 1):
        arrived(zrq.at[i], zs_sem.at[i], zr_sem.at[i])
        value = value + unpack(zrq[i], zlong, WIDE)
    sum_ref[...] = unfold(value, kr)

    for d in range(chips):
        come = lax.rem(chip + chips - d, chips) * 2 + 1 - core
        arrived(gf.at[come], xs_sem.at[d], xr_sem.at[d])
    for i in range(nr):
        block = jnp.concatenate([unpack(gf[i, j], gcols) for j in range(lots)], axis=0)
        for k in range(3 * slots):
            g_ref[k * width + i * share : k * width + (i + 1) * share, :] = block[k * share : (k + 1) * share, :]

    for made in sent:
        made.wait_send()

    @pl.when(is_source)
    def _():
        for e in range(1, ratio):
            for made in panel_copies(e):
                made.wait_send()

    @pl.when(jnp.logical_not(same_chip))
    def _():
        for e in range(ratio):
            forward_copy(e)[1].wait_send()


def finish(sum_ref, g_ref, top_ref, piv_ref, pc_ref, pd_ref, cu_ref, cc_ref, cd_ref):
    width = top_ref.shape[0]
    slots = width // BLOCK
    top = top_ref[...]
    value = sum_ref[...]
    parent = value[:, :width]
    high, low = split(parent)
    pc_ref[...] = -parent
    cc_ref[...] = dot(high, top) + dot(low, top) - value[:, width:]

    def square(i):
        return jnp.concatenate(
            [g_ref[(i * slots + j) * width : (i * slots + j + 1) * width, :] for j in range(slots)], axis=1
        )

    diag = piv_ref[0] + square(0)
    pd_ref[...] = diag
    cross = square(1)
    high, low = split(diag)
    upper = cross.T - (dot(high, top) + dot(low, top))
    cu_ref[...] = upper
    high, low = split(upper)
    cross_high, cross_low = split(cross)
    cd_ref[...] = (
        piv_ref[1] - (dot_t(top, high) + dot_t(top, low))
        - (dot(cross_high, top) + dot(cross_low, top)) + square(2)
    )


def shards(nr, nc, inverse_block, tile_mask, factor, panel_mask, child_top, pivots):
    rows, cols = inverse_block.shape
    width = factor.shape[2]
    ratio = nc // nr
    kr = rows // nc
    small = 3 * width * width // BLOCK
    grows = small // nr
    lots = nc if grows % (GROUP * nc) == 0 else 1
    gcols = grows // lots
    dma = pltpu.SemaphoreType.DMA
    vmem, anywhere = pl.BlockSpec(memory_space=pltpu.VMEM), pl.BlockSpec(memory_space=pl.ANY)
    square = jax.ShapeDtypeStruct((width, width), F32)
    column = jax.ShapeDtypeStruct((kr, width), F32)
    others = max(ratio - 1, 1)
    chips, hrows = nr // 2, 2 * width // nr
    hlong, zlong = hrows * cols // BLOCK, kr * 2 * width // BLOCK
    I16 = jnp.int16
    summed, small_sums = pl.pallas_call(
        functools.partial(kernel, nr, nc, lots),
        out_shape=(pltpu.VMEM((kr, 2 * width), F32), pltpu.VMEM((small, BLOCK), F32)),
        in_specs=[anywhere] * 4,
        out_specs=(vmem,) * 2,
        scratch_shapes=[
            pltpu.VMEM(inverse_block.shape, BF16),
            pltpu.VMEM(tile_mask.shape[::-1], jnp.int32),
            pltpu.VMEM(factor.shape, BF16),
            pltpu.VMEM(panel_mask.shape, jnp.int32),
            pltpu.VMEM((rows, cols), BF16),
            pltpu.VMEM((rows, 2 * width), BF16),
            pltpu.VMEM((2 * width, rows), BF16),
            pltpu.VMEM((rows, 2 * width), BF16),
            pltpu.VMEM((others, nr, kr, cols), BF16),
            pltpu.VMEM((nr, kr, 2 * width), F32),
            pltpu.VMEM((nr - 1, packed(zlong, WIDE), BLOCK), I16),
            pltpu.VMEM((nr - 1, packed(zlong, WIDE), BLOCK), I16),
            pltpu.VMEM((2 * width, cols), F32),
            pltpu.VMEM((chips, packed(hlong, WIDE), BLOCK), I16),
            pltpu.VMEM((chips, packed(hlong, WIDE), BLOCK), I16),
            pltpu.VMEM((chips - 1, packed(hlong, WIDE), BLOCK), I16),
            pltpu.VMEM((chips - 1, packed(hlong, WIDE), BLOCK), I16),
            pltpu.VMEM((lots, packed(gcols), BLOCK), I16),
            pltpu.VMEM((nc, packed(gcols), BLOCK), I16),
            pltpu.VMEM((nr, lots, packed(gcols), BLOCK), I16),
            dma((4,)),
            dma((2 * ratio, max(nr // 2, 1))), dma((2 * ratio,)), dma((ratio,)),
            dma((others, nr)), dma((others, nr)),
            dma((nr - 1,)), dma((nr - 1,)),
            dma((1,)), dma((1,)), dma((chips - 1,)), dma((chips - 1,)),
            dma((nc - 1,)), dma((nc - 1,)), dma((nc - 1,)), dma((nc - 1,)),
            dma((chips - 1,)), dma((chips - 1,)), dma((chips,)), dma((chips,)),
        ],
        compiler_params=pltpu.CompilerParams(
            collective_id=0, has_side_effects=True, vmem_limit_bytes=56 * 1024 * 1024
        ),
    )(inverse_block, tile_mask.T, factor, panel_mask)
    return pl.pallas_call(
        finish,
        out_shape=(column, square, square, column, square),
        in_specs=[vmem] * 4,
        out_specs=(vmem,) * 5,
        compiler_params=pltpu.CompilerParams(vmem_limit_bytes=24 * 1024 * 1024),
    )(summed, small_sums, child_top, pivots)


def solution(mesh):
    in_specs = (P("row", "col"), P("row", "col"), P(None, "row", None), P(None, "row"), P(), P())
    out_specs = (P(("row", "col"), None), P(), P(), P(("row", "col"), None), P())
    body = functools.partial(shards, mesh.shape["row"], mesh.shape["col"])
    return jax.shard_map(body, mesh=mesh, in_specs=in_specs, out_specs=out_specs, check_vma=False)
```

```python
import functools

import jax
import jax.numpy as jnp
from jax import lax
from jax.experimental import pallas as pl
from jax.experimental.pallas import tpu as pltpu
from jax.sharding import PartitionSpec as P

BLOCK = 128
GROUP = 16
WIDE = 32
MESH = pl.DeviceIdType.MESH
F32 = jnp.float32
BF16 = jnp.bfloat16


def split(a):
    high = a.astype(BF16)
    return high, (a - high.astype(F32)).astype(BF16)


def dot(a, b):
    return jnp.dot(a, b, preferred_element_type=F32)


def dot_t(a, b):
    return lax.dot_general(a, b, (((0,), (0,)), ((), ())), preferred_element_type=F32)


def packed(rows, group=GROUP):
    return rows + -(-(rows // group) // 16) * 16


def pack(a, group=GROUP):
    groups = a.shape[0] // group
    parts = a.reshape(groups, group, a.shape[1])
    largest = jnp.maximum(jnp.max(jnp.abs(parts), axis=1), 1e-30)
    power = jnp.ceil(jnp.log2(largest) - 14.99)
    whole = jnp.round(parts * jnp.exp2(-power)[:, None, :]).astype(jnp.int32)
    whole = whole.reshape(a.shape).astype(jnp.int16)
    padding = packed(a.shape[0], group) - a.shape[0] - groups
    if padding:
        power = jnp.concatenate([power, jnp.zeros((padding, a.shape[1]), F32)], axis=0)
    return jnp.concatenate([whole, power.astype(jnp.int32).astype(jnp.int16)], axis=0)


def unpack(held, rows, group=GROUP):
    groups = rows // group
    scale = jnp.exp2(held[rows:].astype(jnp.int32).astype(F32))[:groups]
    parts = held[:rows].astype(jnp.int32).astype(F32).reshape(groups, group, held.shape[1])
    return (parts * scale[:, None, :]).reshape(rows, held.shape[1])


def fold(a):
    return jnp.concatenate([a[:, j : j + BLOCK] for j in range(0, a.shape[1], BLOCK)], axis=0)


def unfold(a, rows):
    return jnp.concatenate([a[i : i + rows] for i in range(0, a.shape[0], rows)], axis=1)


def kernel(
    nr, nc, lots, m_any, tm_any, f_any, pm_any, sum_ref, g_ref,
    m_ref, tm_ref, f_ref, pm_ref, mk, jown, jt, jz, mx, q, zq, zrq,
    hf, h1, h1r, h2, h2r, gt, gc, gf, in_sem,
    ps_sem, pr_sem, fs_sem, ms_sem, mr_sem, zs_sem, zr_sem,
    as_sem, ar_sem, es_sem, er_sem, bs_sem, br_sem, cs_sem, cr_sem, ds_sem, dr_sem, xs_sem, xr_sem,
):
    r, c = lax.axis_index("row"), lax.axis_index("col")
    ratio = nc // nr
    rows, cols = m_ref.shape
    x, z = lax.rem(c, ratio), lax.div(c, ratio)
    width = f_ref.shape[2]
    kr = rows // nc
    qr = cols // 2
    grows = g_ref.shape[0] // nr
    shared = lots == 1
    gcols = grows // lots
    share = width // nr
    hrows = 2 * share
    hlong = hrows * cols // BLOCK
    zlong = kr * 2 * width // BLOCK
    half = nr // 2
    pair, side = lax.div(z, 2), lax.rem(z, 2)

    def pair_dest(m, which):
        return lax.rem(pair + m, half) * 2 + which

    order = [pair_dest(m, 1 - side) for m in range(1, half)]
    order += [pair_dest(m, side) for m in range(1, half)]
    order += [pair_dest(0, 1 - side), z]
    chip, core = lax.div(r, 2), lax.rem(r, 2)
    chips = nr // 2
    mate = chip * 2 + 1 - core
    is_source = r == z
    same_chip = chip == lax.div(z, 2)
    sent = []

    loads = [
        pltpu.make_async_copy(there, here, in_sem.at[i])
        for i, (there, here) in enumerate(
            ((pm_any, pm_ref), (f_any, f_ref), (tm_any, tm_ref), (m_any, m_ref))
        )
    ]
    for load in loads:
        load.start()

    def copy(src, dst, send, recv, row, col):
        return pltpu.make_async_remote_copy(
            src_ref=src, dst_ref=dst, send_sem=send, recv_sem=recv,
            device_id=(row, col), device_id_type=MESH,
        )

    def start(src, dst, send, recv, row, col):
        made = copy(src, dst, send, recv, row, col)
        made.start()
        sent.append(made)

    def arrived(dst, send, recv):
        copy(dst, dst, send, recv, r, c).wait_recv()

    def at(ref, first, count):
        return ref.at[pl.ds(pl.multiple_of(first, 16), count)]

    barrier = pltpu.get_barrier_semaphore()
    for d in range(1, nr):
        pl.semaphore_signal(
            barrier, inc=1, device_id=(lax.rem(r + d, nr), c), device_id_type=MESH
        )
    for d in range(1, nc):
        pl.semaphore_signal(
            barrier, inc=1, device_id=(r, lax.rem(c + d, nc)), device_id_type=MESH
        )
    loads[0].wait()
    loads[1].wait()
    for b in range(rows // BLOCK):
        part = slice(b * BLOCK, (b + 1) * BLOCK)
        for s in range(2):
            keep = pm_ref[s : s + 1, b : b + 1].astype(F32)
            jown[part, s * width : (s + 1) * width] = (f_ref[s, part, :].astype(F32) * keep).astype(BF16)
    pl.semaphore_wait(barrier, nr + nc - 2)

    def piece(ref, e, h):
        part_of = lax.rem(x + e, ratio)
        return at(ref, (part_of * 2 + h) * qr, qr)

    def panel_copies(e):
        made = []
        for h in range(2):
            i = 2 * e + h
            for d in range(1, chips):
                to = lax.rem(chip + d, chips) * 2 + h
                made.append(
                    copy(piece(jown, e, h), piece(jz, e, h), ps_sem.at[i, d], pr_sem.at[i], to, c)
                )
            made.append(
                copy(piece(jown, e, h), piece(jz, e, h), ps_sem.at[i, 0], pr_sem.at[i], mate, c)
            )
        return made

    def forward_copy(e):
        part_of = lax.rem(x + e, ratio)
        part = at(jz, (part_of * 2 + core) * qr, qr)
        i = 2 * e + core
        return part, copy(part, part, fs_sem.at[e], pr_sem.at[i], mate, c)

    def panels_forward(e):
        @pl.when(jnp.logical_not(same_chip))
        def _():
            part, made = forward_copy(e)
            arrived(part, fs_sem.at[e], pr_sem.at[2 * e + core])
            made.start()

    def panels_arrive(e):
        @pl.when(jnp.logical_and(jnp.logical_not(is_source), same_chip))
        def _():
            for h in range(2):
                arrived(piece(jz, e, h), ps_sem.at[2 * e + h, 0], pr_sem.at[2 * e + h])

        @pl.when(jnp.logical_not(same_chip))
        def _():
            other = at(jz, (lax.rem(x + e, ratio) * 2 + 1 - core) * qr, qr)
            arrived(other, fs_sem.at[e], pr_sem.at[2 * e + 1 - core])

    @pl.when(is_source)
    def _():
        for made in panel_copies(0):
            made.start()

    loads[2].wait()
    loads[3].wait()
    for b in range(rows // BLOCK):
        for j in range(cols // BLOCK):
            tile = (slice(b * BLOCK, (b + 1) * BLOCK), slice(j * BLOCK, (j + 1) * BLOCK))
            keep = tm_ref[j : j + 1, b : b + 1].astype(F32)
            mk[tile] = (m_ref[tile].astype(F32) * keep).astype(BF16)
    for e, g in enumerate(order):
        for d in range(1, ratio):
            xx = lax.rem(x + d, ratio)
            start(
                at(mk, (g * ratio + xx) * kr, kr), mx.at[d - 1, e],
                ms_sem.at[d - 1, e], mr_sem.at[d - 1, e], r, z * ratio + xx,
            )

    jt[...] = jown[...].T
    for i in range(2):
        for k in range(2 * width // 256):
            part = slice(k * 256, (k + 1) * 256)
            span = slice(i * cols // 2, (i + 1) * cols // 2)
            hf[part, span] = dot(jt[part, :], mk[:, span])

    def chunk(to):
        first = pl.multiple_of(to * share, 16)
        return fold(jnp.concatenate([hf[pl.ds(first, share), :], hf[pl.ds(width + first, share), :]], axis=0))

    for i in range(chips):
        h1[i] = pack(chunk(i * 2 + 1 - core), WIDE)
    start(h1, h1r, as_sem.at[0], ar_sem.at[0], mate, c)
    arrived(h1r, as_sem.at[0], ar_sem.at[0])
    for d in range(1, chips):
        there = lax.rem(chip + d, chips)
        h2[d - 1] = pack(chunk(there * 2 + core) + unpack(h1r[there], hlong, WIDE), WIDE)
        start(h2.at[d - 1], h2r.at[d - 1], es_sem.at[d - 1], er_sem.at[d - 1], there * 2 + core, c)

    @pl.when(is_source)
    def _():
        jz[...] = jown[...]
        for made in panel_copies(0):
            made.wait_send()
        for e in range(1, ratio):
            for made in panel_copies(e):
                made.start()

    total = chunk(r) + unpack(h1r[chip], hlong, WIDE)

    panels_forward(0)
    panels_arrive(0)
    near = jz[pl.ds(pl.multiple_of(x * cols, cols), cols), :]
    for e, g in enumerate(order):
        q[e] = dot(mk[pl.ds(pl.multiple_of((g * ratio + x) * kr, 16), kr), :], near)

    for d in range(1, chips):
        arrived(h2r.at[d - 1], es_sem.at[d - 1], er_sem.at[d - 1])
        total = total + unpack(h2r[d - 1], hlong, WIDE)
    total = unfold(total, hrows)
    high, low = split(total)
    parent = dot(high[:share], near[:, :width]) + dot(low[:share], near[:, :width])
    both = dot(high[share:], near) + dot(low[share:], near)
    slots = width // BLOCK
    pieces = [parent[:, j * BLOCK : (j + 1) * BLOCK] for j in range(slots)]
    pieces += [both[:, j * BLOCK : (j + 1) * BLOCK] for j in range(2 * slots)]
    total = jnp.concatenate(pieces, axis=0)

    for i in range(lots):
        gt[i] = pack(total[i * gcols : (i + 1) * gcols, :])
    for d in range(1, nc):
        to = lax.rem(c + d, nc)
        start(gt.at[0 if shared else to], gc.at[c], bs_sem.at[d - 1], br_sem.at[d - 1], r, to)
    place = 0 if shared else c
    gc[pl.ds(c, 1)] = gt[pl.ds(place, 1)]

    for e in range(1, ratio):
        panels_forward(e)
    for d in range(1, nc):
        come = lax.rem(c + nc - d, nc)
        arrived(gc.at[come], bs_sem.at[d - 1], br_sem.at[d - 1])
    total = unpack(gc[0], gcols)
    for i in range(1, nc):
        total = total + unpack(gc[i], gcols)
    gf[r, place] = pack(total)
    if not shared:
        for d in range(1, nc):
            to = lax.rem(c + d, nc)
            start(gf.at[r, c], gf.at[r, c], cs_sem.at[d - 1], cr_sem.at[d - 1], r, to)

    for e in range(1, ratio):
        panels_arrive(e)

    def send_rows(value, i, to):
        zq[i] = pack(value, WIDE)
        start(zq.at[i], zrq.at[i], zs_sem.at[i], zr_sem.at[i], r, to * ratio + x)

    for e in range(nr):
        value = q[e]
        for d in range(1, ratio):
            arrived(mx.at[d - 1, e], ms_sem.at[d - 1, e], mr_sem.at[d - 1, e])
            other = lax.rem(x - d + ratio, ratio)
            value = value + dot(mx[d - 1, e], jz[pl.ds(pl.multiple_of(other * cols, cols), cols), :])
        if e < half - 1:
            send_rows(fold(value), e, pair_dest(0, 1 - side))
        elif e == nr - 2:
            send_rows(fold(value), half - 1, pair_dest(0, 1 - side))
        else:
            q[e] = value
    if not shared:
        for d in range(1, nc):
            come = lax.rem(c + nc - d, nc)
            arrived(gf.at[r, come], cs_sem.at[d - 1], cr_sem.at[d - 1])
    for d in range(1, chips):
        to = lax.rem(chip + d, chips) * 2 + core
        start(gf.at[r], gf.at[r], ds_sem.at[d - 1], dr_sem.at[d - 1], to, c)
    start(gf.at[r], gf.at[r], xs_sem.at[0], xr_sem.at[0], mate, c)
    def restore(line):
        block = jnp.concatenate([unpack(gf[line, j], gcols) for j in range(lots)], axis=0)
        for k in range(3 * slots):
            place_of = pl.multiple_of(k * width + line * share, 16)
            g_ref[pl.ds(place_of, share), :] = block[k * share : (k + 1) * share, :]

    restore(r)
    for m in range(1, half):
        arrived(zrq.at[m - 1], zs_sem.at[m - 1], zr_sem.at[m - 1])
        value = fold(q[half + m - 2]) + unpack(zrq[m - 1], zlong, WIDE)
        send_rows(value, half + m - 1, pair_dest(m, side))

    for d in range(1, chips):
        come = lax.rem(chip + chips - d, chips) * 2 + core
        arrived(gf.at[come], ds_sem.at[d - 1], dr_sem.at[d - 1])
        start(gf.at[come], gf.at[come], xs_sem.at[d], xr_sem.at[d], mate, c)
        restore(come)

    value = fold(q[nr - 1])
    for i in range(half - 1, nr - 1):
        arrived(zrq.at[i], zs_sem.at[i], zr_sem.at[i])
        value = value + unpack(zrq[i], zlong, WIDE)
    sum_ref[...] = unfold(value, kr)

    for d in range(chips):
        come = lax.rem(chip + chips - d, chips) * 2 + 1 - core
        arrived(gf.at[come], xs_sem.at[d], xr_sem.at[d])
        restore(come)

    for made in sent:
        made.wait_send()

    @pl.when(is_source)
    def _():
        for e in range(1, ratio):
            for made in panel_copies(e):
                made.wait_send()

    @pl.when(jnp.logical_not(same_chip))
    def _():
        for e in range(ratio):
            forward_copy(e)[1].wait_send()


def finish(sum_ref, g_ref, top_ref, piv_ref, pc_ref, pd_ref, cu_ref, cc_ref, cd_ref):
    width = top_ref.shape[0]
    slots = width // BLOCK
    top = top_ref[...]
    value = sum_ref[...]
    parent = value[:, :width]
    high, low = split(parent)
    pc_ref[...] = -parent
    cc_ref[...] = dot(high, top) + dot(low, top) - value[:, width:]

    def square(i):
        return jnp.concatenate(
            [g_ref[(i * slots + j) * width : (i * slots + j + 1) * width, :] for j in range(slots)], axis=1
        )

    diag = piv_ref[0] + square(0)
    pd_ref[...] = diag
    cross = square(1)
    high, low = split(diag)
    upper = cross.T - (dot(high, top) + dot(low, top))
    cu_ref[...] = upper
    high, low = split(upper)
    cross_high, cross_low = split(cross)
    cd_ref[...] = (
        piv_ref[1] - (dot_t(top, high) + dot_t(top, low))
        - (dot(cross_high, top) + dot(cross_low, top)) + square(2)
    )


def shards(nr, nc, inverse_block, tile_mask, factor, panel_mask, child_top, pivots):
    rows, cols = inverse_block.shape
    width = factor.shape[2]
    ratio = nc // nr
    kr = rows // nc
    small = 3 * width * width // BLOCK
    grows = small // nr
    lots = nc if grows % (GROUP * nc) == 0 else 1
    gcols = grows // lots
    dma = pltpu.SemaphoreType.DMA
    vmem, anywhere = pl.BlockSpec(memory_space=pltpu.VMEM), pl.BlockSpec(memory_space=pl.ANY)
    square = jax.ShapeDtypeStruct((width, width), F32)
    column = jax.ShapeDtypeStruct((kr, width), F32)
    others = max(ratio - 1, 1)
    chips, hrows = nr // 2, 2 * width // nr
    hlong, zlong = hrows * cols // BLOCK, kr * 2 * width // BLOCK
    I16 = jnp.int16
    summed, small_sums = pl.pallas_call(
        functools.partial(kernel, nr, nc, lots),
        out_shape=(pltpu.VMEM((kr, 2 * width), F32), pltpu.VMEM((small, BLOCK), F32)),
        in_specs=[anywhere] * 4,
        out_specs=(vmem,) * 2,
        scratch_shapes=[
            pltpu.VMEM(inverse_block.shape, BF16),
            pltpu.VMEM(tile_mask.shape[::-1], jnp.int32),
            pltpu.VMEM(factor.shape, BF16),
            pltpu.VMEM(panel_mask.shape, jnp.int32),
            pltpu.VMEM((rows, cols), BF16),
            pltpu.VMEM((rows, 2 * width), BF16),
            pltpu.VMEM((2 * width, rows), BF16),
            pltpu.VMEM((rows, 2 * width), BF16),
            pltpu.VMEM((others, nr, kr, cols), BF16),
            pltpu.VMEM((nr, kr, 2 * width), F32),
            pltpu.VMEM((nr - 1, packed(zlong, WIDE), BLOCK), I16),
            pltpu.VMEM((nr - 1, packed(zlong, WIDE), BLOCK), I16),
            pltpu.VMEM((2 * width, cols), F32),
            pltpu.VMEM((chips, packed(hlong, WIDE), BLOCK), I16),
            pltpu.VMEM((chips, packed(hlong, WIDE), BLOCK), I16),
            pltpu.VMEM((chips - 1, packed(hlong, WIDE), BLOCK), I16),
            pltpu.VMEM((chips - 1, packed(hlong, WIDE), BLOCK), I16),
            pltpu.VMEM((lots, packed(gcols), BLOCK), I16),
            pltpu.VMEM((nc, packed(gcols), BLOCK), I16),
            pltpu.VMEM((nr, lots, packed(gcols), BLOCK), I16),
            dma((4,)),
            dma((2 * ratio, max(nr // 2, 1))), dma((2 * ratio,)), dma((ratio,)),
            dma((others, nr)), dma((others, nr)),
            dma((nr - 1,)), dma((nr - 1,)),
            dma((1,)), dma((1,)), dma((chips - 1,)), dma((chips - 1,)),
            dma((nc - 1,)), dma((nc - 1,)), dma((nc - 1,)), dma((nc - 1,)),
            dma((chips - 1,)), dma((chips - 1,)), dma((chips,)), dma((chips,)),
        ],
        compiler_params=pltpu.CompilerParams(
            collective_id=0, has_side_effects=True, vmem_limit_bytes=56 * 1024 * 1024
        ),
    )(inverse_block, tile_mask.T, factor, panel_mask)
    return pl.pallas_call(
        finish,
        out_shape=(column, square, square, column, square),
        in_specs=[vmem] * 4,
        out_specs=(vmem,) * 5,
        compiler_params=pltpu.CompilerParams(vmem_limit_bytes=24 * 1024 * 1024),
    )(summed, small_sums, child_top, pivots)


def solution(mesh):
    in_specs = (P("row", "col"), P("row", "col"), P(None, "row", None), P(None, "row"), P(), P())
    out_specs = (P(("row", "col"), None), P(), P(), P(("row", "col"), None), P())
    body = functools.partial(shards, mesh.shape["row"], mesh.shape["col"])
    return jax.shard_map(body, mesh=mesh, in_specs=in_specs, out_specs=out_specs, check_vma=False)
```

```python
import functools

import jax
import jax.numpy as jnp
from jax import lax
from jax.experimental import pallas as pl
from jax.experimental.pallas import tpu as pltpu
from jax.sharding import PartitionSpec as P

BLOCK = 128
GROUP = 16
WIDE = 32
MESH = pl.DeviceIdType.MESH
F32 = jnp.float32
BF16 = jnp.bfloat16


def split(a):
    high = a.astype(BF16)
    return high, (a - high.astype(F32)).astype(BF16)


def dot(a, b):
    return jnp.dot(a, b, preferred_element_type=F32)


def dot_t(a, b):
    return lax.dot_general(a, b, (((0,), (0,)), ((), ())), preferred_element_type=F32)


def packed(rows, group=GROUP):
    return rows + -(-(rows // group) // 16) * 16


def pack(a, group=GROUP):
    groups = a.shape[0] // group
    parts = a.reshape(groups, group, a.shape[1])
    largest = jnp.maximum(jnp.max(jnp.abs(parts), axis=1), 1e-30)
    power = jnp.ceil(jnp.log2(largest) - 14.99)
    whole = jnp.round(parts * jnp.exp2(-power)[:, None, :]).astype(jnp.int32)
    whole = whole.reshape(a.shape).astype(jnp.int16)
    padding = packed(a.shape[0], group) - a.shape[0] - groups
    if padding:
        power = jnp.concatenate([power, jnp.zeros((padding, a.shape[1]), F32)], axis=0)
    return jnp.concatenate([whole, power.astype(jnp.int32).astype(jnp.int16)], axis=0)


def unpack(held, rows, group=GROUP):
    groups = rows // group
    scale = jnp.exp2(held[rows:].astype(jnp.int32).astype(F32))[:groups]
    parts = held[:rows].astype(jnp.int32).astype(F32).reshape(groups, group, held.shape[1])
    return (parts * scale[:, None, :]).reshape(rows, held.shape[1])


def fold(a):
    return jnp.concatenate([a[:, j : j + BLOCK] for j in range(0, a.shape[1], BLOCK)], axis=0)


def unfold(a, rows):
    return jnp.concatenate([a[i : i + rows] for i in range(0, a.shape[0], rows)], axis=1)


def kernel(
    nr, nc, lots, m_any, tm_any, f_any, pm_any, sum_ref, g_ref,
    m_ref, tm_ref, f_ref, pm_ref, mk, jown, jt, jz, mx, q, zq, zrq,
    hf, h1, h1r, h2, h2r, gt, gc, gf, in_sem,
    ps_sem, pr_sem, fs_sem, ms_sem, mr_sem, zs_sem, zr_sem,
    as_sem, ar_sem, es_sem, er_sem, bs_sem, br_sem, cs_sem, cr_sem, ds_sem, dr_sem, xs_sem, xr_sem,
):
    r, c = lax.axis_index("row"), lax.axis_index("col")
    ratio = nc // nr
    rows, cols = m_ref.shape
    x, z = lax.rem(c, ratio), lax.div(c, ratio)
    width = f_ref.shape[2]
    kr = rows // nc
    qr = cols // 2
    grows = g_ref.shape[0] // nr
    shared = lots == 1
    gcols = grows // lots
    share = width // nr
    hrows = 2 * share
    hlong = hrows * cols // BLOCK
    zlong = kr * 2 * width // BLOCK
    half = nr // 2
    pair, side = lax.div(z, 2), lax.rem(z, 2)

    def pair_dest(m, which):
        return lax.rem(pair + m, half) * 2 + which

    order = [pair_dest(m, 1 - side) for m in range(1, half)]
    order += [pair_dest(m, side) for m in range(1, half)]
    order += [pair_dest(0, 1 - side), z]
    chip, core = lax.div(r, 2), lax.rem(r, 2)
    chips = nr // 2
    mate = chip * 2 + 1 - core
    is_source = r == z
    same_chip = chip == lax.div(z, 2)
    sent = []

    loads = [
        pltpu.make_async_copy(there, here, in_sem.at[i])
        for i, (there, here) in enumerate(
            ((pm_any, pm_ref), (f_any, f_ref), (tm_any, tm_ref), (m_any, m_ref))
        )
    ]
    for load in loads:
        load.start()

    def copy(src, dst, send, recv, row, col):
        return pltpu.make_async_remote_copy(
            src_ref=src, dst_ref=dst, send_sem=send, recv_sem=recv,
            device_id=(row, col), device_id_type=MESH,
        )

    def start(src, dst, send, recv, row, col):
        made = copy(src, dst, send, recv, row, col)
        made.start()
        sent.append(made)

    def arrived(dst, send, recv):
        copy(dst, dst, send, recv, r, c).wait_recv()

    def at(ref, first, count):
        return ref.at[pl.ds(pl.multiple_of(first, 16), count)]

    barrier = pltpu.get_barrier_semaphore()
    for d in range(1, nr):
        pl.semaphore_signal(
            barrier, inc=1, device_id=(lax.rem(r + d, nr), c), device_id_type=MESH
        )
    for d in range(1, nc):
        pl.semaphore_signal(
            barrier, inc=1, device_id=(r, lax.rem(c + d, nc)), device_id_type=MESH
        )
    loads[0].wait()
    loads[1].wait()
    for b in range(rows // BLOCK):
        part = slice(b * BLOCK, (b + 1) * BLOCK)
        for s in range(2):
            keep = pm_ref[s : s + 1, b : b + 1].astype(F32)
            jown[part, s * width : (s + 1) * width] = (f_ref[s, part, :].astype(F32) * keep).astype(BF16)
    pl.semaphore_wait(barrier, nr + nc - 2)

    def piece(ref, e, h):
        part_of = lax.rem(x + e, ratio)
        return at(ref, (part_of * 2 + h) * qr, qr)

    def panel_copies(e):
        made = []
        for h in range(2):
            i = 2 * e + h
            for d in range(1, chips):
                to = lax.rem(chip + d, chips) * 2 + h
                made.append(
                    copy(piece(jown, e, h), piece(jz, e, h), ps_sem.at[i, d], pr_sem.at[i], to, c)
                )
            made.append(
                copy(piece(jown, e, h), piece(jz, e, h), ps_sem.at[i, 0], pr_sem.at[i], mate, c)
            )
        return made

    def forward_copy(e):
        part_of = lax.rem(x + e, ratio)
        part = at(jz, (part_of * 2 + core) * qr, qr)
        i = 2 * e + core
        return part, copy(part, part, fs_sem.at[e], pr_sem.at[i], mate, c)

    def panels_forward(e):
        @pl.when(jnp.logical_not(same_chip))
        def _():
            part, made = forward_copy(e)
            arrived(part, fs_sem.at[e], pr_sem.at[2 * e + core])
            made.start()

    def panels_arrive(e):
        @pl.when(jnp.logical_and(jnp.logical_not(is_source), same_chip))
        def _():
            for h in range(2):
                arrived(piece(jz, e, h), ps_sem.at[2 * e + h, 0], pr_sem.at[2 * e + h])

        @pl.when(jnp.logical_not(same_chip))
        def _():
            other = at(jz, (lax.rem(x + e, ratio) * 2 + 1 - core) * qr, qr)
            arrived(other, fs_sem.at[e], pr_sem.at[2 * e + 1 - core])

    @pl.when(is_source)
    def _():
        for e in range(ratio):
            for made in panel_copies(e):
                made.start()

    loads[2].wait()
    loads[3].wait()
    for b in range(rows // BLOCK):
        for j in range(cols // BLOCK):
            tile = (slice(b * BLOCK, (b + 1) * BLOCK), slice(j * BLOCK, (j + 1) * BLOCK))
            keep = tm_ref[j : j + 1, b : b + 1].astype(F32)
            mk[tile] = (m_ref[tile].astype(F32) * keep).astype(BF16)
    for e, g in enumerate(order):
        for d in range(1, ratio):
            xx = lax.rem(x + d, ratio)
            start(
                at(mk, (g * ratio + xx) * kr, kr), mx.at[d - 1, e],
                ms_sem.at[d - 1, e], mr_sem.at[d - 1, e], r, z * ratio + xx,
            )

    jt[...] = jown[...].T
    for i in range(2):
        for k in range(2 * width // 256):
            part = slice(k * 256, (k + 1) * 256)
            span = slice(i * cols // 2, (i + 1) * cols // 2)
            hf[part, span] = dot(jt[part, :], mk[:, span])

    def chunk(to):
        first = pl.multiple_of(to * share, 16)
        return fold(jnp.concatenate([hf[pl.ds(first, share), :], hf[pl.ds(width + first, share), :]], axis=0))

    for i in range(chips):
        h1[i] = pack(chunk(i * 2 + 1 - core), WIDE)
    start(h1, h1r, as_sem.at[0], ar_sem.at[0], mate, c)
    arrived(h1r, as_sem.at[0], ar_sem.at[0])
    for d in range(1, chips):
        there = lax.rem(chip + d, chips)
        h2[d - 1] = pack(chunk(there * 2 + core) + unpack(h1r[there], hlong, WIDE), WIDE)
        start(h2.at[d - 1], h2r.at[d - 1], es_sem.at[d - 1], er_sem.at[d - 1], there * 2 + core, c)

    @pl.when(is_source)
    def _():
        jz[...] = jown[...]

    total = chunk(r) + unpack(h1r[chip], hlong, WIDE)

    panels_forward(0)
    panels_arrive(0)
    near = jz[pl.ds(pl.multiple_of(x * cols, cols), cols), :]
    for e, g in enumerate(order):
        q[e] = dot(mk[pl.ds(pl.multiple_of((g * ratio + x) * kr, 16), kr), :], near)

    for d in range(1, chips):
        arrived(h2r.at[d - 1], es_sem.at[d - 1], er_sem.at[d - 1])
        total = total + unpack(h2r[d - 1], hlong, WIDE)
    total = unfold(total, hrows)
    high, low = split(total)
    parent = dot(high[:share], near[:, :width]) + dot(low[:share], near[:, :width])
    both = dot(high[share:], near) + dot(low[share:], near)
    slots = width // BLOCK
    pieces = [parent[:, j * BLOCK : (j + 1) * BLOCK] for j in range(slots)]
    pieces += [both[:, j * BLOCK : (j + 1) * BLOCK] for j in range(2 * slots)]
    total = jnp.concatenate(pieces, axis=0)

    for i in range(lots):
        gt[i] = pack(total[i * gcols : (i + 1) * gcols, :])
    for d in range(1, nc):
        to = lax.rem(c + d, nc)
        start(gt.at[0 if shared else to], gc.at[c], bs_sem.at[d - 1], br_sem.at[d - 1], r, to)
    place = 0 if shared else c
    gc[pl.ds(c, 1)] = gt[pl.ds(place, 1)]

    for e in range(1, ratio):
        panels_forward(e)
    for d in range(1, nc):
        come = lax.rem(c + nc - d, nc)
        arrived(gc.at[come], bs_sem.at[d - 1], br_sem.at[d - 1])
    total = unpack(gc[0], gcols)
    for i in range(1, nc):
        total = total + unpack(gc[i], gcols)
    gf[r, place] = pack(total)
    if not shared:
        for d in range(1, nc):
            to = lax.rem(c + d, nc)
            start(gf.at[r, c], gf.at[r, c], cs_sem.at[d - 1], cr_sem.at[d - 1], r, to)

    for e in range(1, ratio):
        panels_arrive(e)

    def send_rows(value, i, to):
        zq[i] = pack(value, WIDE)
        start(zq.at[i], zrq.at[i], zs_sem.at[i], zr_sem.at[i], r, to * ratio + x)

    for e in range(nr):
        value = q[e]
        for d in range(1, ratio):
            arrived(mx.at[d - 1, e], ms_sem.at[d - 1, e], mr_sem.at[d - 1, e])
            other = lax.rem(x - d + ratio, ratio)
            value = value + dot(mx[d - 1, e], jz[pl.ds(pl.multiple_of(other * cols, cols), cols), :])
        if e < half - 1:
            send_rows(fold(value), e, pair_dest(0, 1 - side))
        elif e == nr - 2:
            send_rows(fold(value), half - 1, pair_dest(0, 1 - side))
        else:
            q[e] = value
    if not shared:
        for d in range(1, nc):
            come = lax.rem(c + nc - d, nc)
            arrived(gf.at[r, come], cs_sem.at[d - 1], cr_sem.at[d - 1])
    for d in range(1, chips):
        to = lax.rem(chip + d, chips) * 2 + core
        start(gf.at[r], gf.at[r], ds_sem.at[d - 1], dr_sem.at[d - 1], to, c)
    start(gf.at[r], gf.at[r], xs_sem.at[0], xr_sem.at[0], mate, c)
    def restore(line):
        block = jnp.concatenate([unpack(gf[line, j], gcols) for j in range(lots)], axis=0)
        for k in range(3 * slots):
            place_of = pl.multiple_of(k * width + line * share, 16)
            g_ref[pl.ds(place_of, share), :] = block[k * share : (k + 1) * share, :]

    restore(r)
    for m in range(1, half):
        arrived(zrq.at[m - 1], zs_sem.at[m - 1], zr_sem.at[m - 1])
        value = fold(q[half + m - 2]) + unpack(zrq[m - 1], zlong, WIDE)
        send_rows(value, half + m - 1, pair_dest(m, side))

    for d in range(1, chips):
        come = lax.rem(chip + chips - d, chips) * 2 + core
        arrived(gf.at[come], ds_sem.at[d - 1], dr_sem.at[d - 1])
        start(gf.at[come], gf.at[come], xs_sem.at[d], xr_sem.at[d], mate, c)
        restore(come)

    value = fold(q[nr - 1])
    for i in range(half - 1, nr - 1):
        arrived(zrq.at[i], zs_sem.at[i], zr_sem.at[i])
        value = value + unpack(zrq[i], zlong, WIDE)
    sum_ref[...] = unfold(value, kr)

    for d in range(chips):
        come = lax.rem(chip + chips - d, chips) * 2 + 1 - core
        arrived(gf.at[come], xs_sem.at[d], xr_sem.at[d])
        restore(come)

    for made in sent:
        made.wait_send()

    @pl.when(is_source)
    def _():
        for e in range(ratio):
            for made in panel_copies(e):
                made.wait_send()

    @pl.when(jnp.logical_not(same_chip))
    def _():
        for e in range(ratio):
            forward_copy(e)[1].wait_send()


def finish(sum_ref, g_ref, top_ref, piv_ref, pc_ref, pd_ref, cu_ref, cc_ref, cd_ref):
    width = top_ref.shape[0]
    slots = width // BLOCK
    top = top_ref[...]
    value = sum_ref[...]
    parent = value[:, :width]
    high, low = split(parent)
    pc_ref[...] = -parent
    cc_ref[...] = dot(high, top) + dot(low, top) - value[:, width:]

    def square(i):
        return jnp.concatenate(
            [g_ref[(i * slots + j) * width : (i * slots + j + 1) * width, :] for j in range(slots)], axis=1
        )

    diag = piv_ref[0] + square(0)
    pd_ref[...] = diag
    cross = square(1)
    high, low = split(diag)
    upper = cross.T - (dot(high, top) + dot(low, top))
    cu_ref[...] = upper
    high, low = split(upper)
    cross_high, cross_low = split(cross)
    cd_ref[...] = (
        piv_ref[1] - (dot_t(top, high) + dot_t(top, low))
        - (dot(cross_high, top) + dot(cross_low, top)) + square(2)
    )


def shards(nr, nc, inverse_block, tile_mask, factor, panel_mask, child_top, pivots):
    rows, cols = inverse_block.shape
    width = factor.shape[2]
    ratio = nc // nr
    kr = rows // nc
    small = 3 * width * width // BLOCK
    grows = small // nr
    lots = nc if grows % (GROUP * nc) == 0 else 1
    gcols = grows // lots
    dma = pltpu.SemaphoreType.DMA
    vmem, anywhere = pl.BlockSpec(memory_space=pltpu.VMEM), pl.BlockSpec(memory_space=pl.ANY)
    square = jax.ShapeDtypeStruct((width, width), F32)
    column = jax.ShapeDtypeStruct((kr, width), F32)
    others = max(ratio - 1, 1)
    chips, hrows = nr // 2, 2 * width // nr
    hlong, zlong = hrows * cols // BLOCK, kr * 2 * width // BLOCK
    I16 = jnp.int16
    summed, small_sums = pl.pallas_call(
        functools.partial(kernel, nr, nc, lots),
        out_shape=(pltpu.VMEM((kr, 2 * width), F32), pltpu.VMEM((small, BLOCK), F32)),
        in_specs=[anywhere] * 4,
        out_specs=(vmem,) * 2,
        scratch_shapes=[
            pltpu.VMEM(inverse_block.shape, BF16),
            pltpu.VMEM(tile_mask.shape[::-1], jnp.int32),
            pltpu.VMEM(factor.shape, BF16),
            pltpu.VMEM(panel_mask.shape, jnp.int32),
            pltpu.VMEM((rows, cols), BF16),
            pltpu.VMEM((rows, 2 * width), BF16),
            pltpu.VMEM((2 * width, rows), BF16),
            pltpu.VMEM((rows, 2 * width), BF16),
            pltpu.VMEM((others, nr, kr, cols), BF16),
            pltpu.VMEM((nr, kr, 2 * width), F32),
            pltpu.VMEM((nr - 1, packed(zlong, WIDE), BLOCK), I16),
            pltpu.VMEM((nr - 1, packed(zlong, WIDE), BLOCK), I16),
            pltpu.VMEM((2 * width, cols), F32),
            pltpu.VMEM((chips, packed(hlong, WIDE), BLOCK), I16),
            pltpu.VMEM((chips, packed(hlong, WIDE), BLOCK), I16),
            pltpu.VMEM((chips - 1, packed(hlong, WIDE), BLOCK), I16),
            pltpu.VMEM((chips - 1, packed(hlong, WIDE), BLOCK), I16),
            pltpu.VMEM((lots, packed(gcols), BLOCK), I16),
            pltpu.VMEM((nc, packed(gcols), BLOCK), I16),
            pltpu.VMEM((nr, lots, packed(gcols), BLOCK), I16),
            dma((4,)),
            dma((2 * ratio, max(nr // 2, 1))), dma((2 * ratio,)), dma((ratio,)),
            dma((others, nr)), dma((others, nr)),
            dma((nr - 1,)), dma((nr - 1,)),
            dma((1,)), dma((1,)), dma((chips - 1,)), dma((chips - 1,)),
            dma((nc - 1,)), dma((nc - 1,)), dma((nc - 1,)), dma((nc - 1,)),
            dma((chips - 1,)), dma((chips - 1,)), dma((chips,)), dma((chips,)),
        ],
        compiler_params=pltpu.CompilerParams(
            collective_id=0, has_side_effects=True, vmem_limit_bytes=56 * 1024 * 1024
        ),
    )(inverse_block, tile_mask.T, factor, panel_mask)
    return pl.pallas_call(
        finish,
        out_shape=(column, square, square, column, square),
        in_specs=[vmem] * 4,
        out_specs=(vmem,) * 5,
        compiler_params=pltpu.CompilerParams(vmem_limit_bytes=24 * 1024 * 1024),
    )(summed, small_sums, child_top, pivots)


def solution(mesh):
    in_specs = (P("row", "col"), P("row", "col"), P(None, "row", None), P(None, "row"), P(), P())
    out_specs = (P(("row", "col"), None), P(), P(), P(("row", "col"), None), P())
    body = functools.partial(shards, mesh.shape["row"], mesh.shape["col"])
    return jax.shard_map(body, mesh=mesh, in_specs=in_specs, out_specs=out_specs, check_vma=False)
```
